32 devices in a mesh: dp: 4 (over z), expert: 8 (over y, x, core).
Axes of the slice: x: 2, y: 2, z: 4, core: 2. Of those that a mesh axis runs over, the one named last changes fastest.
Arguments:
- tokens: bfloat16 [4096, 3584], P(('dp', 'expert')), may hold values from -6 to 6
- expert_ids: int32 [4096, 1], P(('dp', 'expert')), may hold values from 0 to 7; in each aligned block of 128 rows (0 to 127, 128 to 255, ...) at most 32 rows name the same one
- gates: bfloat16 [4096], P(('dp', 'expert')), may hold values from 0.19921875 to 1
- cotangent: bfloat16 [4096, 1024], P(('dp', 'expert')), may hold values from -6 to 6
- weights: bfloat16 [8, 3584, 1024], P('expert'), may hold values from -0.09375 to 0.09375
Outputs:
- hidden: bfloat16 [4096, 1024], P(('dp', 'expert'))
- grad: float32 [8, 3584, 1024], P('expert', 'dp')
The draws below stay inside these ranges and needn't reach their ends.
Inputs may be any that keep to these rules, and one draw needn't show every extreme that they name: `expert_ids`: among the 128 tokens of one device at most 32 name one expert; some device and expert reach 32 in every draw.
All inputs are finite; a program needn't handle non-finite values.
Results may differ from the reference program's by a relative error of at most 0.0029.
Values may be sent and summed in bfloat16 or wider, within the bound.
No kernel may reach another device: no remote copies, remote signals or barrier semaphores. Data moves between devices by JAX's collectives and lax.ppermute only.
A program may use at most 64 MiB of HBM per device.

```python
import math
import jax
import jax.numpy as jnp
import numpy as np
from jax import lax

D = 3584
H = 1024
TOK_DEV = 128
CAP = 32
EXPERTS = 8
TOKENS = 4096
N_DP = 4
N_EXPERT = 8


def shard_levels(own_key, dims, pieces, low, high):
    loudness, own = 1.0, jax.random.fold_in(own_key, 6)
    for axis_at, blocks in pieces:
        heights = jnp.exp(jax.random.uniform(jax.random.fold_in(own, axis_at), (blocks,), jnp.float32, low / len(pieces), high / len(pieces)))
        loudness = loudness * jnp.repeat(heights, dims[axis_at] // blocks).reshape([-1 if axis == axis_at else 1 for axis in range(len(dims))])
    return loudness


def assign_block(key, own, number, rows, count, top, reach, slope):
    sequence = jax.random.permutation(key, count)
    packed, usual = portions_of(count, rows * top, reach, slope, True), portions_of(count, rows * top, reach, slope, False)
    places = jnp.arange(count)

    def named(lengths, turn):
        used = int((lengths > 0).sum())
        fixed = max(1, used // 4)
        moved = fixed + (places - fixed + turn * (used - fixed)) % max(1, count - fixed)
        return jnp.zeros((count,), jnp.int32).at[sequence[jnp.where(places < fixed, places, moved)]].set(jnp.asarray(lengths, jnp.int32))

    lengths = jnp.where(number % 4 == 0, named(packed, number // 4), named(usual, number - number // 4 - 1))
    mixed = jax.random.permutation(jax.random.fold_in(own, 3), count)
    donor, sink = mixed[0:count // 2 * 2:2], mixed[1:count // 2 * 2:2]
    room = jnp.minimum(lengths[donor] - 1, reach - lengths[sink]) // 2
    room = jnp.where((donor == sequence[0]) | (sink == sequence[0]) | (lengths[sink] == 0), 0, jnp.maximum(room, 0))
    moved = jax.random.randint(jax.random.fold_in(own, 4), (count // 2,), 0, 1 << 20) % (room + 1)
    lengths = lengths.at[donor].add(-moved).at[sink].add(moved)
    labels = jnp.searchsorted(jnp.cumsum(lengths), jnp.arange(rows * top), side="right").astype(jnp.int32)
    grid = labels.reshape(top, rows).T
    grid = grid[jax.random.permutation(jax.random.fold_in(own, 1), rows)]
    turn = jax.random.randint(jax.random.fold_in(own, 2), (rows, 1), 0, top)
    return jnp.take_along_axis(grid, (jnp.arange(top)[None, :] + turn) % top, axis=1)


def portions_of(amount, total, limit, lean, full):
    portions = [(1 << 20) // math.isqrt(standing ** lean) + 1 for standing in range(1, amount + 1)]
    largest = limit if full else min(limit, max(-(-total // amount), total * portions[0] // sum(portions)))
    least = 1 if total - largest >= amount - 1 else 0
    given, rest = [largest] + [least] * (amount - 1), total - largest - least * (amount - 1)
    while rest > 0:
        free = [i for i in range(1, amount) if given[i] < largest] or [i for i in range(1, amount) if given[i] < limit]
        whole, budget = sum([portions[i] for i in free]), rest
        for i in free:
            addition = min(limit - given[i], max(1, budget * portions[i] // whole), rest)
            given[i] = given[i] + addition
            rest = rest - addition
    return np.array(given)


def gaussian(key, extent, spread, most, split=(), kind=jnp.bfloat16):
    values = spread * jax.random.normal(key, extent, jnp.float32)
    if split:
        values = values * shard_levels(key, extent, split, -0.22, 0.18)
    return jnp.clip(values, -most, most).astype(kind)


def setup_inputs(seed: int = 0) -> dict:
    streams_of = jax.random.split(jax.random.key(seed), 6)
    tokens = gaussian(streams_of[0], (TOKENS, D), 1.0, 6.0, ((0, 32),))
    expert_ids_keys = jax.random.split(jax.random.fold_in(streams_of[1], 1), TOKENS // TOK_DEV)
    expert_ids_turns = jax.random.permutation(jax.random.fold_in(streams_of[1], 3), TOKENS // TOK_DEV)
    expert_ids = jax.vmap(lambda own, number: assign_block(jax.random.fold_in(streams_of[1], 2), own, number, TOK_DEV, EXPERTS, 1, CAP, 2))(expert_ids_keys, expert_ids_turns).reshape((TOKENS, 1))
    gates = jnp.clip(0.19921875 + 0.80078125 * jax.random.uniform(streams_of[2], (TOKENS,), jnp.float32) ** shard_levels(streams_of[2], (TOKENS,), ((0, 32),), -0.2, 0.2), 0.19921875, 1.0).astype(jnp.bfloat16)
    cotangent = gaussian(streams_of[3], (TOKENS, H), 1.0, 6.0, ((0, 32),))
    weights = gaussian(streams_of[4], (EXPERTS, D, H), D ** -0.5, 0.09375, ((0, 8),))
    return dict(tokens=tokens, expert_ids=expert_ids, gates=gates, cotangent=cotangent, weights=weights)


def reference(tokens, expert_ids, gates, cotangent, weights):
    ndev = TOKENS // TOK_DEV
    ids = expert_ids[:, 0].reshape(ndev, TOK_DEV)
    onehot = (ids[:, :, None] == jnp.arange(EXPERTS, dtype=jnp.int32)[None, None, :]).astype(jnp.int32)
    before = jnp.cumsum(onehot, axis=1) - onehot
    rank = jnp.sum(before * onehot, axis=2).astype(jnp.int32)
    device = jnp.broadcast_to(jnp.arange(ndev, dtype=jnp.int32)[:, None], (ndev, TOK_DEV))
    group = device // N_EXPERT
    source = device % N_EXPERT
    tok_index = jnp.arange(TOKENS, dtype=jnp.int32).reshape(ndev, TOK_DEV)
    table = jnp.full((N_DP, EXPERTS, N_EXPERT, CAP), -1, jnp.int32)
    table = table.at[group, ids, source, rank].set(tok_index)
    table = table.reshape(N_DP, EXPERTS, N_EXPERT * CAP)

    def per_expert(args):
        index, weight = args
        valid = index >= 0
        safe = jnp.where(valid, index, 0)
        rows = jnp.where(valid[:, None], tokens[safe], jnp.zeros((), jnp.bfloat16))
        gate = jnp.where(valid, gates[safe].astype(jnp.float32), 0.0)[:, None]
        cots = jnp.where(valid[:, None], cotangent[safe].astype(jnp.float32), 0.0)
        pre = jnp.dot(rows, weight, preferred_element_type=jnp.float32)
        sig = jax.nn.sigmoid(pre)
        hval = (gate * pre * sig).astype(jnp.bfloat16)
        dpre = (cots * gate * sig * (1.0 + pre * (1.0 - sig))).astype(jnp.bfloat16)
        part = jnp.dot(rows.T, dpre, preferred_element_type=jnp.float32)
        return hval, part

    def per_group(total, index):
        hvals, parts = lax.map(per_expert, (index, weights))
        return total + parts, hvals

    grad, hvals = lax.scan(per_group, jnp.zeros((EXPERTS, D, H), jnp.float32), table)
    flat = hvals.reshape(N_DP * EXPERTS * N_EXPERT * CAP, H)
    where = ((group * EXPERTS + ids) * N_EXPERT + source) * CAP + rank
    hidden = flat[where.reshape(TOKENS)]
    return hidden, grad
```

```python
import functools

import jax
import jax.numpy as jnp
from jax import lax
from jax.experimental import pallas as pl
from jax.experimental.pallas import tpu as pltpu
from jax.sharding import PartitionSpec as P

LANES = 128


def swap(value, axis, offset):
    count = lax.axis_size(axis)
    return lax.ppermute(value, axis, [(i, i ^ offset) for i in range(count)])


def placing_of(ids, me, experts, slots, parts):
    count = ids.shape[1]
    part = slots // parts
    named = lax.broadcasted_iota(jnp.int32, (experts, count), 0) == ids
    earlier = (
        lax.broadcasted_iota(jnp.int32, (count, count), 0)
        < lax.broadcasted_iota(jnp.int32, (count, count), 1)
    ).astype(jnp.bfloat16)
    before = jnp.dot(named.astype(jnp.bfloat16), earlier, preferred_element_type=jnp.float32)
    rank = jnp.sum(jnp.where(named, before, 0.0), axis=0, keepdims=True).astype(jnp.int32)
    piece = sum(((rank >= part * p).astype(jnp.int32) for p in range(1, parts)), jnp.zeros_like(rank))
    row = (piece * experts + (ids ^ me)) * part + rank - piece * part
    return lax.broadcasted_iota(jnp.int32, (experts * slots, count), 0) == row


def place_kernel(experts, slots, parts, me_ref, ids_ref, gates_ref, tokens_ref, cots_ref, *outs):
    placing = placing_of(ids_ref[...], me_ref[0], experts, slots, parts)
    one_hot = placing.astype(jnp.bfloat16)
    width, inner = tokens_ref.shape[1], cots_ref.shape[1]
    gate = jnp.sum(
        jnp.where(placing, gates_ref[...].astype(jnp.float32), 0.0), axis=1, keepdims=True
    )
    gate = jnp.broadcast_to(gate, (gate.shape[0], LANES)).astype(jnp.bfloat16)
    cots = jnp.dot(one_hot, cots_ref[...], preferred_element_type=jnp.float32).astype(jnp.bfloat16)
    rows = jnp.dot(one_hot, tokens_ref[...], preferred_element_type=jnp.float32).astype(
        jnp.bfloat16
    )
    part = slots // parts
    for i, out in enumerate(outs):
        here = slice(i * part, (i + 1) * part)
        out[:, :width] = rows[here]
        out[:, width : width + inner] = cots[here]
        out[:, width + inner :] = gate[here]


def share_kernel(experts, slots, parts, groups, me_ref, *refs):
    ids, tokens, outs = refs[:groups], refs[groups : 2 * groups], refs[2 * groups :]
    part = slots // parts
    for g in range(groups):
        one_hot = placing_of(ids[g][...], me_ref[0], experts, slots, parts).astype(jnp.bfloat16)
        rows = jnp.dot(one_hot, tokens[g][...], preferred_element_type=jnp.float32).astype(
            jnp.bfloat16
        )
        for p in range(parts):
            for k in range(experts):
                i = p * experts + k
                outs[k][(g * parts + p) * part : (g * parts + p + 1) * part] = rows[
                    i * part : (i + 1) * part
                ]


def vmem(count):
    return [pl.BlockSpec(memory_space=pltpu.VMEM)] * count


def on_device(tokens, expert_ids, gates, cotangent, weights):
    experts = lax.axis_size("expert")
    members = lax.axis_size("dp")
    me = lax.axis_index("expert")
    group = lax.axis_index("dp")
    count, width = tokens.shape
    inner = cotangent.shape[1]
    share = width // members
    slots = max(2, 2 * count // experts)
    parts = 2 if slots % 32 == 0 else 1
    part = slots // parts
    wide = width + inner + LANES
    me_ref = me.reshape(1)
    ids = expert_ids.reshape(1, count)

    everyone = lax.all_gather(ids, "dp", axis=0, tiled=True)
    shares = []
    for k in range(1, members):
        cut = lax.dynamic_slice_in_dim(tokens, (group ^ k) * share, share, 1)
        shares.append(swap(cut, "dp", k))
    others = [lax.dynamic_slice_in_dim(everyone, group ^ k, 1, 0) for k in range(1, members)]

    placed = pl.pallas_call(
        functools.partial(place_kernel, experts, slots, parts),
        out_shape=[jax.ShapeDtypeStruct((part, wide), jnp.bfloat16)] * (parts * experts),
        in_specs=[pl.BlockSpec(memory_space=pltpu.SMEM)] + vmem(4),
        out_specs=vmem(parts * experts),
        compiler_params=pltpu.CompilerParams(vmem_limit_bytes=32 << 20),
        name="place",
    )(me_ref, ids, gates.reshape(1, count), tokens, cotangent)

    received = []
    for p in range(parts):
        blocks = placed[p * experts : (p + 1) * experts]
        got = [blocks[0]] + [None] * (experts - 1)
        for k in reversed(range(1, experts)):
            got[k] = swap(blocks[k], "expert", k)
        received.append(jnp.concatenate(got, axis=0))

    weight = weights[0]
    activation, dpres, own = [], [], []
    for p in range(parts):
        rows = received[p][:, :width]
        cots = received[p][:, width : width + inner].astype(jnp.float32)
        gate = received[p][:, width + inner : width + inner + 1].astype(jnp.float32)
        pre = jnp.dot(rows, weight, preferred_element_type=jnp.float32)
        sig = jax.nn.sigmoid(pre)
        activation.append((gate * pre * sig).astype(jnp.bfloat16))
        dpres.append((cots * gate * sig * (1.0 + pre * (1.0 - sig))).astype(jnp.bfloat16))
        own.append(lax.dynamic_slice_in_dim(rows, group * share, share, 1))

    groups = members - 1
    blocks = pl.pallas_call(
        functools.partial(share_kernel, experts, slots, parts, groups),
        out_shape=[jax.ShapeDtypeStruct((groups * slots, share), jnp.bfloat16)] * experts,
        in_specs=[pl.BlockSpec(memory_space=pltpu.SMEM)] + vmem(2 * groups),
        out_specs=vmem(experts),
        compiler_params=pltpu.CompilerParams(vmem_limit_bytes=32 << 20),
        name="place_shares",
    )(me_ref, *others, *shares)
    lefts = [blocks[0]] + [swap(blocks[k], "expert", k) for k in range(1, experts)]
    lefts = jnp.stack(lefts).reshape(experts, groups, parts, part, share)

    gathered = [[None] * parts for _ in range(groups)]
    for p in range(parts):
        if members == 4:
            mine = dpres[p]
            first = swap(mine, "dp", 1)
            middle = [(1, 2), (2, 1)]
            outward = [(1, 0), (2, 3)]
            across = lax.ppermute(mine, "dp", middle)
            far = lax.ppermute(first, "dp", middle)
            ends = (group == 0) | (group == 3)
            out_near = lax.ppermute(across, "dp", outward)
            out_far = lax.ppermute(far, "dp", outward)
            second = jnp.where(ends, out_near, far)
            third = jnp.where(ends, out_far, across)
            gathered[0][p], gathered[1][p], gathered[2][p] = first, second, third
        else:
            for k in range(1, members):
                gathered[k - 1][p] = swap(dpres[p], "dp", k)

    back = []
    for p in range(parts):
        act = activation[p].reshape(experts, part, inner)
        back += [act[0]] + [swap(act[k], "expert", k) for k in range(1, experts)]
    returned = jnp.concatenate(back, axis=0)
    placing = placing_of(ids, me, experts, slots, parts).astype(jnp.bfloat16)
    hidden = lax.dot_general(
        placing, returned, (((0,), (0,)), ((), ())), preferred_element_type=jnp.float32
    ).astype(jnp.bfloat16)

    left, right = list(own), list(dpres)
    for j in range(groups):
        for p in range(parts):
            left.append(lefts[:, j, p].reshape(experts * part, share))
            right.append(gathered[j][p])
    grad = lax.dot_general(
        jnp.concatenate(left, axis=0),
        jnp.concatenate(right, axis=0),
        (((0,), (0,)), ((), ())),
        preferred_element_type=jnp.float32,
    )
    return (hidden, grad[None])


def solution(mesh):
    return jax.shard_map(
        on_device,
        mesh=mesh,
        in_specs=(
            P(("dp", "expert"), None),
            P(("dp", "expert"), None),
            P(("dp", "expert")),
            P(("dp", "expert"), None),
            P("expert", None, None),
        ),
        out_specs=(P(("dp", "expert"), None), P("expert", "dp", None)),
        check_vma=False,
    )
```

```python
import functools

import jax
import jax.numpy as jnp
from jax import lax
from jax.experimental import pallas as pl
from jax.experimental.pallas import tpu as pltpu
from jax.sharding import PartitionSpec as P

LANES = 128
TAIL = 16
F32, BF16 = jnp.float32, jnp.bfloat16
HBM = pl.BlockSpec(memory_space=pltpu.HBM)
VMEM = pl.BlockSpec(memory_space=pltpu.VMEM)
ANY = pl.BlockSpec(memory_space=pl.ANY)


def limit(mebibytes):
    return pltpu.CompilerParams(vmem_limit_bytes=mebibytes << 20)


def struct(*shape):
    return jax.ShapeDtypeStruct(shape, BF16)


def swap(value, axis, offset):
    count = lax.axis_size(axis)
    return lax.ppermute(value, axis, [(i, i ^ offset) for i in range(count)])


def hold_kernel(*refs):
    pass


def after(values, *others):
    return pl.pallas_call(
        hold_kernel,
        out_shape=[jax.ShapeDtypeStruct(value.shape, value.dtype) for value in values],
        in_specs=[ANY] * (len(values) + len(others)),
        out_specs=[ANY] * len(values),
        input_output_aliases={i: i for i in range(len(values))},
        compiler_params=limit(1),
        name="hold",
    )(*values, *others)


def fetch(pairs, sems):
    copies = [pltpu.make_async_copy(a, b, sems.at[i]) for i, (a, b) in enumerate(pairs)]
    for copy in copies:
        copy.start()
    return copies


def placing_of(ids, me, step, experts, slots):
    count = ids.shape[1]
    named = lax.broadcasted_iota(jnp.int32, (experts, count), 0) == ids
    earlier = (
        lax.broadcasted_iota(jnp.int32, (count, count), 0)
        < lax.broadcasted_iota(jnp.int32, (count, count), 1)
    ).astype(BF16)
    before = jnp.dot(named.astype(BF16), earlier, preferred_element_type=F32)
    rank = jnp.sum(jnp.where(named, before, 0.0), axis=0, keepdims=True).astype(jnp.int32)
    offset = ids ^ me
    row = jnp.where(offset % step == 0, (offset // step) * slots + rank, -1)
    return lax.broadcasted_iota(jnp.int32, (experts // step * slots, count), 0) == row


def columns(ref, index, share):
    if share % LANES == 0:
        return ref[:, pl.ds(pl.multiple_of(index * share, LANES), share)]
    value = ref[...]
    total = jnp.zeros((value.shape[0], share), value.dtype)
    for g in range(value.shape[1] // share):
        total = jnp.where(index == g, value[:, g * share : (g + 1) * share], total)
    return total


def place_kernel(sizes, *refs):
    experts, slots = sizes
    hbm, outs, scratch, sems = refs[:4], refs[4:-5], refs[-5:-1], refs[-1]
    for copy in fetch(list(zip(hbm, scratch)), sems):
        copy.wait()
    outs, cuts = outs[:experts], outs[experts:]
    ids_ref, gates_ref, cots_ref, tokens_ref = scratch
    count, width = tokens_ref.shape
    inner = cots_ref.shape[1]
    names = jnp.broadcast_to(ids_ref[...].astype(F32), (TAIL, count)).astype(BF16)
    group = lax.axis_index("dp")
    for k, out in enumerate(cuts):
        share = out.shape[1]
        out[:count, :] = columns(tokens_ref, group ^ (k + 1), share)
        out[count:, :count] = names
        if share > count:
            out[count:, count:] = jnp.zeros((TAIL, share - count), BF16)
    placing = placing_of(ids_ref[...], lax.axis_index("expert"), 1, experts, slots)
    one_hot = placing.astype(BF16)
    gate = jnp.sum(jnp.where(placing, gates_ref[...].astype(F32), 0.0), axis=1, keepdims=True)
    gate = jnp.broadcast_to(gate, (gate.shape[0], LANES)).astype(BF16)
    cots = jnp.dot(one_hot, cots_ref[...], preferred_element_type=F32).astype(BF16)
    rows = jnp.dot(one_hot, tokens_ref[...], preferred_element_type=F32).astype(BF16)
    for k, out in enumerate(outs):
        here = slice(k * slots, (k + 1) * slots)
        out[:, :width] = rows[here]
        out[:, width : width + inner] = cots[here]
        out[:, width + inner :] = gate[here]


def forward_kernel(sizes, weight_ref, *rest):
    experts, width, inner, share, parts = sizes
    pairs = experts // 2
    blocks, rest = rest[:experts], rest[experts + pairs :]
    sent, rest = rest[:pairs], rest[pairs:]
    dpre_refs, (own_ref, all_ref) = rest[:parts], rest[parts:]
    slots = blocks[0].shape[0]
    for k, block in enumerate(blocks):
        all_ref[k * slots : (k + 1) * slots, :] = block[...]
    pre = jnp.dot(all_ref[:, :width], weight_ref[0], preferred_element_type=F32)
    cots = all_ref[:, width : width + inner].astype(F32)
    gate = all_ref[:, width + inner :][:, :1].astype(F32)
    sig = jax.nn.sigmoid(pre)
    gated = gate * sig
    dpre = (cots * gated * (1.0 + pre * (1.0 - sig))).astype(BF16)
    height = dpre.shape[0] // parts
    for p, out in enumerate(dpre_refs):
        out[...] = dpre[p * height : (p + 1) * height]
    act = (gated * pre).astype(BF16)
    for j, out in enumerate(sent):
        out[:, out.shape[1] - inner :] = act[2 * j * slots : 2 * (j + 1) * slots]
    own_ref[...] = columns(all_ref.at[:, :width], lax.axis_index("dp"), share)


def share_kernel(sizes, *refs):
    experts, slots, groups, count = sizes
    pairs = experts // 2
    mine, theirs, outs = refs[:groups], refs[groups : 2 * groups], refs[-pairs:]
    share = mine[0].shape[1]
    for out in outs:
        out[:, groups * share :] = jnp.zeros_like(out[:, groups * share :])
    me = lax.axis_index("expert")
    for g in range(groups):
        placed = []
        for block in (mine[g], theirs[g]):
            ids = block[count:, :count][:1].astype(F32).astype(jnp.int32)
            one_hot = placing_of(ids, me, 2, experts, slots).astype(BF16)
            placed.append(
                jnp.dot(one_hot, block[:count, :], preferred_element_type=F32).astype(BF16)
            )
        for j, out in enumerate(outs):
            here = slice(j * slots, (j + 1) * slots)
            out[:, g * share : (g + 1) * share] = jnp.concatenate([p[here] for p in placed], axis=0)


def split_kernel(slots, inner, *refs):
    *blocks, out_ref = refs
    for j, block in enumerate(blocks):
        out_ref[j * slots : (j + 1) * slots] = block[slots:, block.shape[1] - inner :]


def unplace_kernel(sizes, ids_ref, theirs_ref, *refs):
    experts, slots = sizes
    *blocks, out_ref = refs
    inner = out_ref.shape[1]
    me = lax.axis_index("expert")
    mine = [block[:slots, block.shape[1] - inner :] for block in blocks]
    total = jnp.zeros(out_ref.shape, F32)
    for r, value in enumerate((jnp.concatenate(mine, axis=0), theirs_ref[...])):
        one_hot = placing_of(ids_ref[...], me ^ r, 2, experts, slots).astype(BF16)
        total = total + lax.dot_general(
            one_hot, value, (((0,), (0,)), ((), ())), preferred_element_type=F32
        )
    out_ref[...] = total.astype(BF16)


def turn_kernel(groups, own_ref, *refs):
    *blocks, out_ref = refs
    share, rows = out_ref.shape[0], own_ref.shape[0]
    out_ref[:, :rows] = own_ref[...].T
    for g in range(groups):
        value = [block[:, g * share : (g + 1) * share] for block in blocks]
        out_ref[:, (g + 1) * rows : (g + 2) * rows] = jnp.concatenate(value, axis=0).T


def sum_kernel(groups, left_ref, *refs):
    pieces, (out_ref, right_ref) = refs[:-2], refs[-2:]
    rows = left_ref.shape[1] // 4
    at = 0
    for piece in pieces:
        right_ref[at : at + piece.shape[0], :] = piece[...]
        at += piece.shape[0]
    total = jnp.zeros(out_ref.shape, F32)
    for i, g in enumerate(groups):
        total = total + jnp.dot(
            left_ref[:, g * rows : (g + 1) * rows],
            right_ref[i * rows : (i + 1) * rows, :],
            preferred_element_type=F32,
        )
    out_ref[...] = total


def grad_kernel(group, left_ref, before_ref, *refs):
    pieces, (out_hbm, right_ref, total_ref, sems) = refs[:-4], refs[-4:]
    rows = left_ref.shape[1] // 4
    at = 0
    for piece in pieces:
        right_ref[at : at + piece.shape[0], :] = piece[...]
        at += piece.shape[0]
    steps, tall = total_ref.shape[:2]
    copies = []
    for i in range(steps):
        here = slice(i * tall, (i + 1) * tall)
        total_ref[i] = before_ref[here, :] + jnp.dot(
            left_ref[here, group * rows : (group + 1) * rows],
            right_ref[...],
            preferred_element_type=F32,
        )
        copies.append(pltpu.make_async_copy(total_ref.at[i], out_hbm.at[here, :], sems.at[i]))
        copies[-1].start()
    for copy in copies:
        copy.wait()


def on_device(tokens, expert_ids, gates, cotangent, weights):
    experts, members = lax.axis_size("expert"), lax.axis_size("dp")
    group = lax.axis_index("dp")
    pairs, groups = experts // 2, members - 1
    count, width = tokens.shape
    inner = cotangent.shape[1]
    share = width // members
    slots = max(2, 2 * count // experts)
    rows = experts * slots
    wide = width + inner + LANES
    chain = slots % 16 == 0 and share % LANES == 0 and members == 4
    ids, gates = expert_ids.reshape(1, count), gates.reshape(1, count)

    mine = (ids, gates, cotangent, tokens)
    placed = pl.pallas_call(
        functools.partial(place_kernel, (experts, slots)),
        out_shape=[struct(slots, wide)] * experts + [struct(count + TAIL, share)] * groups,
        in_specs=[HBM] * 4,
        out_specs=[VMEM] * (experts + groups),
        scratch_shapes=[pltpu.VMEM(value.shape, value.dtype) for value in mine]
        + [pltpu.SemaphoreType.DMA((4,))],
        compiler_params=limit(BIG),
        name="place",
    )(*mine)
    placed, cuts = placed[:experts], placed[experts:]
    got = list(placed)
    for k in range(2, experts, 2):
        got[k] = swap(placed[k], "expert", k)
    for k, value in zip(range(1, experts, 2), after(placed[1::2], *got[2::2])):
        got[k] = swap(value, "expert", k)
    cuts = [swap(cut, "dp", k + 1) for k, cut in enumerate(cuts)]

    sent = pl.pallas_call(
        functools.partial(share_kernel, (experts, slots, groups, count)),
        out_shape=[struct(2 * slots, groups * share + inner)] * pairs,
        in_specs=[VMEM] * (1 + 2 * groups),
        out_specs=[VMEM] * pairs,
        compiler_params=limit(SMALL),
        name="place_shares",
    )(*cuts, *[swap(cut, "expert", 1) for cut in cuts], weights)
    sent, dpres, own = (lambda a: (a[:pairs], list(a[pairs:-1]), a[-1]))(
        pl.pallas_call(
            functools.partial(forward_kernel, (experts, width, inner, share, PARTS)),
            out_shape=[struct(2 * slots, groups * share + inner)] * pairs
            + [struct(rows // PARTS, inner)] * PARTS
            + [struct(rows, share)],
            in_specs=[VMEM] * (1 + experts + pairs),
            out_specs=[VMEM] * (1 + pairs + PARTS),
            input_output_aliases={1 + experts + j: j for j in range(pairs)},
            scratch_shapes=[pltpu.VMEM((rows, wide), BF16)],
            compiler_params=limit(SMALL),
            name="forward",
        )(weights, *got, *sent)
    )

    gathered = [[] for _ in range(groups)]
    for value in dpres:
        for k in range(1, members):
            if not (chain and k == 2):
                gathered[k - 1].append(swap(value, "dp", k))
    if chain:
        ends = (group == 0) | (group == 3)
        for value, far in zip(dpres, gathered[2]):
            value = jnp.where(ends, value, far)
            gathered[1].append(lax.ppermute(value, "dp", [(0, 2), (1, 0), (2, 3), (3, 1)]))

    lefts = [sent[0]] + [swap(sent[j], "expert", 2 * j) for j in range(1, pairs)]
    theirs = pl.pallas_call(
        functools.partial(split_kernel, slots, inner),
        out_shape=struct(pairs * slots, inner),
        in_specs=[VMEM] * pairs,
        out_specs=VMEM,
        compiler_params=limit(SMALL),
        name="split",
    )(*lefts)
    hidden = pl.pallas_call(
        functools.partial(unplace_kernel, (experts, slots)),
        out_shape=struct(count, inner),
        in_specs=[VMEM] * (2 + pairs),
        out_specs=VMEM,
        compiler_params=limit(SMALL),
        name="unplace",
    )(ids, swap(theirs, "expert", 1), *lefts)

    if chain:
        left = pl.pallas_call(
            functools.partial(turn_kernel, groups),
            out_shape=struct(share, members * rows),
            in_specs=[VMEM] * (1 + pairs),
            out_specs=VMEM,
            compiler_params=limit(SMALL),
            name="turn",
        )(own, *lefts)
        pieces = [*dpres] + gathered[0] + gathered[2]
        before = pl.pallas_call(
            functools.partial(sum_kernel, (0, 1, 3)),
            out_shape=jax.ShapeDtypeStruct((share, inner), F32),
            in_specs=[VMEM] * (1 + len(pieces)),
            out_specs=VMEM,
            scratch_shapes=[pltpu.VMEM((3 * rows, inner), BF16)],
            compiler_params=limit(SMALL),
            name="sum",
        )(left, *pieces)
        steps = 2
        grad = pl.pallas_call(
            functools.partial(grad_kernel, 2),
            out_shape=jax.ShapeDtypeStruct((share, inner), F32),
            in_specs=[VMEM] * (2 + len(dpres)),
            out_specs=HBM,
            scratch_shapes=[
                pltpu.VMEM((rows, inner), BF16),
                pltpu.VMEM((steps, share // steps, inner), F32),
                pltpu.SemaphoreType.DMA((steps,)),
            ],
            compiler_params=limit(SMALL),
            name="grad",
        )(left, before, *gathered[1])
        return (hidden, grad[None])
    left, right = [own], list(dpres)
    for g in range(groups):
        left += [block[:, g * share : (g + 1) * share] for block in lefts]
        right += gathered[g]
    grad = lax.dot_general(
        jnp.concatenate(left, axis=0),
        jnp.concatenate(right, axis=0),
        (((0,), (0,)), ((), ())),
        preferred_element_type=F32,
    )
    return (hidden, grad[None])


BIG, SMALL, PARTS = 40, 12, 1


def solution(mesh):
    return jax.shard_map(
        on_device,
        mesh=mesh,
        in_specs=(
            P(("dp", "expert"), None),
            P(("dp", "expert"), None),
            P(("dp", "expert")),
            P(("dp", "expert"), None),
            P("expert", None, None),
        ),
        out_specs=(P(("dp", "expert"), None), P("expert", "dp", None)),
        check_vma=False,
    )
```

```python
import functools

import jax
import jax.numpy as jnp
from jax import lax
from jax.experimental import pallas as pl
from jax.experimental.pallas import tpu as pltpu
from jax.sharding import PartitionSpec as P

LANES = 128
TAIL = 16
F32, BF16 = jnp.float32, jnp.bfloat16
HBM = pl.BlockSpec(memory_space=pltpu.HBM)
VMEM = pl.BlockSpec(memory_space=pltpu.VMEM)
ANY = pl.BlockSpec(memory_space=pl.ANY)


def limit(mebibytes):
    return pltpu.CompilerParams(vmem_limit_bytes=mebibytes << 20)


def struct(*shape):
    return jax.ShapeDtypeStruct(shape, BF16)


def swap(value, axis, offset):
    count = lax.axis_size(axis)
    return lax.ppermute(value, axis, [(i, i ^ offset) for i in range(count)])


def hold_kernel(*refs):
    pass


def after(values, *others):
    return pl.pallas_call(
        hold_kernel,
        out_shape=[jax.ShapeDtypeStruct(value.shape, value.dtype) for value in values],
        in_specs=[ANY] * (len(values) + len(others)),
        out_specs=[ANY] * len(values),
        input_output_aliases={i: i for i in range(len(values))},
        compiler_params=limit(1),
        name="hold",
    )(*values, *others)


def fetch(pairs, sems):
    copies = [pltpu.make_async_copy(a, b, sems.at[i]) for i, (a, b) in enumerate(pairs)]
    for copy in copies:
        copy.start()
    return copies


def placing_of(ids, me, step, experts, slots):
    count = ids.shape[1]
    named = lax.broadcasted_iota(jnp.int32, (experts, count), 0) == ids
    earlier = (
        lax.broadcasted_iota(jnp.int32, (count, count), 0)
        < lax.broadcasted_iota(jnp.int32, (count, count), 1)
    ).astype(BF16)
    before = jnp.dot(named.astype(BF16), earlier, preferred_element_type=F32)
    rank = jnp.sum(jnp.where(named, before, 0.0), axis=0, keepdims=True).astype(jnp.int32)
    offset = ids ^ me
    row = jnp.where(offset % step == 0, (offset // step) * slots + rank, -1)
    return lax.broadcasted_iota(jnp.int32, (experts // step * slots, count), 0) == row


def columns(ref, index, share):
    if share % LANES == 0:
        return ref[:, pl.ds(pl.multiple_of(index * share, LANES), share)]
    value = ref[...]
    total = jnp.zeros((value.shape[0], share), value.dtype)
    for g in range(value.shape[1] // share):
        total = jnp.where(index == g, value[:, g * share : (g + 1) * share], total)
    return total


def place_kernel(sizes, *refs):
    experts, slots = sizes
    hbm, outs, scratch, sems = refs[:4], refs[4:-5], refs[-5:-1], refs[-1]
    for copy in fetch(list(zip(hbm, scratch)), sems):
        copy.wait()
    outs, cuts = outs[:experts], outs[experts:]
    ids_ref, gates_ref, cots_ref, tokens_ref = scratch
    count, width = tokens_ref.shape
    inner = cots_ref.shape[1]
    names = jnp.broadcast_to(ids_ref[...].astype(F32), (TAIL, count)).astype(BF16)
    group = lax.axis_index("dp")
    for k, out in enumerate(cuts):
        share = out.shape[1]
        out[:count, :] = columns(tokens_ref, group ^ (k + 1), share)
        out[count:, :count] = names
        if share > count:
            out[count:, count:] = jnp.zeros((TAIL, share - count), BF16)
    placing = placing_of(ids_ref[...], lax.axis_index("expert"), 1, experts, slots)
    one_hot = placing.astype(BF16)
    gate = jnp.sum(jnp.where(placing, gates_ref[...].astype(F32), 0.0), axis=1, keepdims=True)
    gate = jnp.broadcast_to(gate, (gate.shape[0], LANES)).astype(BF16)
    cots = jnp.dot(one_hot, cots_ref[...], preferred_element_type=F32).astype(BF16)
    rows = jnp.dot(one_hot, tokens_ref[...], preferred_element_type=F32).astype(BF16)
    for k, out in enumerate(outs):
        here = slice(k * slots, (k + 1) * slots)
        out[:, :width] = rows[here]
        out[:, width : width + inner] = cots[here]
        out[:, width + inner :] = gate[here]


def touch_kernel(weight_ref, tie, out_ref):
    out_ref[...] = weight_ref[0, :8, :LANES]


def forward_kernel(sizes, weight_ref, *rest):
    experts, width, inner, share = sizes
    blocks, (act_ref, dpre_ref, own_ref, all_ref) = rest[:experts], rest[-4:]
    slots = blocks[0].shape[0]
    for k, block in enumerate(blocks):
        all_ref[k * slots : (k + 1) * slots, :] = block[...]
    pre = jnp.dot(all_ref[:, :width], weight_ref[0], preferred_element_type=F32)
    cots = all_ref[:, width : width + inner].astype(F32)
    gate = all_ref[:, width + inner :][:, :1].astype(F32)
    sig = jax.nn.sigmoid(pre)
    gated = gate * sig
    dpre_ref[...] = (cots * gated * (1.0 + pre * (1.0 - sig))).astype(BF16)
    act_ref[...] = (gated * pre).astype(BF16)
    own_ref[...] = columns(all_ref.at[:, :width], lax.axis_index("dp"), share)


def share_kernel(sizes, *refs):
    experts, slots, groups, count = sizes
    pairs = experts // 2
    mine, theirs, act_ref = refs[:groups], refs[groups : 2 * groups], refs[2 * groups]
    outs = refs[2 * groups + 1 :]
    share = mine[0].shape[1]
    me = lax.axis_index("expert")
    for j, out in enumerate(outs):
        out[:, groups * share :] = act_ref[2 * j * slots : 2 * (j + 1) * slots]
    for g in range(groups):
        placed = []
        for block in (mine[g], theirs[g]):
            ids = block[count:, :count][:1].astype(F32).astype(jnp.int32)
            one_hot = placing_of(ids, me, 2, experts, slots).astype(BF16)
            placed.append(
                jnp.dot(one_hot, block[:count, :], preferred_element_type=F32).astype(BF16)
            )
        for j, out in enumerate(outs):
            here = slice(j * slots, (j + 1) * slots)
            out[:, g * share : (g + 1) * share] = jnp.concatenate([p[here] for p in placed], axis=0)


def split_kernel(slots, inner, *refs):
    *blocks, out_ref = refs
    for j, block in enumerate(blocks):
        out_ref[j * slots : (j + 1) * slots] = block[slots:, block.shape[1] - inner :]


def unplace_kernel(sizes, ids_ref, theirs_ref, *refs):
    experts, slots = sizes
    *blocks, out_ref = refs
    inner = out_ref.shape[1]
    me = lax.axis_index("expert")
    mine = [block[:slots, block.shape[1] - inner :] for block in blocks]
    total = jnp.zeros(out_ref.shape, F32)
    for r, value in enumerate((jnp.concatenate(mine, axis=0), theirs_ref[...])):
        one_hot = placing_of(ids_ref[...], me ^ r, 2, experts, slots).astype(BF16)
        total = total + lax.dot_general(
            one_hot, value, (((0,), (0,)), ((), ())), preferred_element_type=F32
        )
    out_ref[...] = total.astype(BF16)


def turn_kernel(groups, own_ref, *refs):
    *blocks, out_ref = refs
    share, rows = out_ref.shape[0], own_ref.shape[0]
    out_ref[:, :rows] = own_ref[...].T
    for g in range(groups):
        value = [block[:, g * share : (g + 1) * share] for block in blocks]
        out_ref[:, (g + 1) * rows : (g + 2) * rows] = jnp.concatenate(value, axis=0).T


def sum_kernel(groups, left_ref, *refs):
    pieces, (out_ref, right_ref) = refs[:-2], refs[-2:]
    rows = left_ref.shape[1] // 4
    at = 0
    for piece in pieces:
        right_ref[at : at + piece.shape[0], :] = piece[...]
        at += piece.shape[0]
    total = jnp.zeros(out_ref.shape, F32)
    for i, g in enumerate(groups):
        total = total + jnp.dot(
            left_ref[:, g * rows : (g + 1) * rows],
            right_ref[i * rows : (i + 1) * rows, :],
            preferred_element_type=F32,
        )
    out_ref[...] = total


def grad_kernel(group, left_ref, before_ref, *refs):
    pieces, (out_hbm, right_ref, total_ref, sems) = refs[:-4], refs[-4:]
    rows = left_ref.shape[1] // 4
    at = 0
    for piece in pieces:
        right_ref[at : at + piece.shape[0], :] = piece[...]
        at += piece.shape[0]
    steps, tall = total_ref.shape[:2]
    copies = []
    for i in range(steps):
        here = slice(i * tall, (i + 1) * tall)
        total_ref[i] = before_ref[here, :] + jnp.dot(
            left_ref[here, group * rows : (group + 1) * rows],
            right_ref[...],
            preferred_element_type=F32,
        )
        copies.append(pltpu.make_async_copy(total_ref.at[i], out_hbm.at[here, :], sems.at[i]))
        copies[-1].start()
    for copy in copies:
        copy.wait()


def on_device(tokens, expert_ids, gates, cotangent, weights):
    experts, members = lax.axis_size("expert"), lax.axis_size("dp")
    group = lax.axis_index("dp")
    pairs, groups = experts // 2, members - 1
    count, width = tokens.shape
    inner = cotangent.shape[1]
    share = width // members
    slots = max(2, 2 * count // experts)
    rows = experts * slots
    wide = width + inner + LANES
    chain = slots % 16 == 0 and share % LANES == 0 and members == 4
    ids, gates = expert_ids.reshape(1, count), gates.reshape(1, count)

    mine = (ids, gates, cotangent, tokens)
    placed = pl.pallas_call(
        functools.partial(place_kernel, (experts, slots)),
        out_shape=[struct(slots, wide)] * experts + [struct(count + TAIL, share)] * groups,
        in_specs=[HBM] * 4,
        out_specs=[VMEM] * (experts + groups),
        scratch_shapes=[pltpu.VMEM(value.shape, value.dtype) for value in mine]
        + [pltpu.SemaphoreType.DMA((4,))],
        compiler_params=limit(BIG),
        name="place",
    )(*mine)
    placed, cuts = placed[:experts], placed[experts:]
    touched = pl.pallas_call(
        touch_kernel,
        out_shape=struct(8, LANES),
        in_specs=[VMEM, ANY],
        out_specs=VMEM,
        compiler_params=limit(1),
        name="touch",
    )(weights, placed[0])
    got = list(placed)
    for k in range(2, experts, 2):
        got[k] = swap(placed[k], "expert", k)
    later = after(placed[1::2], *got[2::2], *([touched] if TOUCH else []))
    for k, value in zip(range(1, experts, 2), later):
        got[k] = swap(value, "expert", k)
    cuts = [cuts[0], *after([cuts[1]], got[2]), *cuts[2:]] if groups > 1 else cuts
    cuts = [swap(cut, "dp", k + 1) for k, cut in enumerate(cuts)]

    act, dpre, own = pl.pallas_call(
        functools.partial(forward_kernel, (experts, width, inner, share)),
        out_shape=[struct(rows, inner), struct(rows, inner), struct(rows, share)],
        in_specs=[VMEM] * (1 + experts) + [ANY] * groups,
        out_specs=[VMEM] * 3,
        scratch_shapes=[pltpu.VMEM((rows, wide), BF16)],
        compiler_params=limit(SMALL),
        name="forward",
    )(weights, *got, *cuts)
    dpres = [dpre]

    gathered = [[] for _ in range(groups)]
    for value in dpres:
        for k in range(1, members):
            if not (chain and k == 2):
                gathered[k - 1].append(swap(value, "dp", k))
    if chain:
        ends = (group == 0) | (group == 3)
        for value, far in zip(dpres, gathered[2]):
            value = jnp.where(ends, value, far)
            gathered[1].append(lax.ppermute(value, "dp", [(0, 2), (1, 0), (2, 3), (3, 1)]))

    sent = pl.pallas_call(
        functools.partial(share_kernel, (experts, slots, groups, count)),
        out_shape=[struct(2 * slots, groups * share + inner)] * pairs,
        in_specs=[VMEM] * (1 + 2 * groups),
        out_specs=[VMEM] * pairs,
        compiler_params=limit(SMALL),
        name="place_shares",
    )(*cuts, *[swap(cut, "expert", 1) for cut in cuts], act)
    lefts = [sent[0]] + [swap(sent[j], "expert", 2 * j) for j in range(1, pairs)]
    theirs = pl.pallas_call(
        functools.partial(split_kernel, slots, inner),
        out_shape=struct(pairs * slots, inner),
        in_specs=[VMEM] * pairs,
        out_specs=VMEM,
        compiler_params=limit(SMALL),
        name="split",
    )(*lefts)
    hidden = pl.pallas_call(
        functools.partial(unplace_kernel, (experts, slots)),
        out_shape=struct(count, inner),
        in_specs=[VMEM] * (2 + pairs),
        out_specs=VMEM,
        compiler_params=limit(SMALL),
        name="unplace",
    )(ids, swap(theirs, "expert", 1), *lefts)

    if chain:
        left = pl.pallas_call(
            functools.partial(turn_kernel, groups),
            out_shape=struct(share, members * rows),
            in_specs=[VMEM] * (1 + pairs),
            out_specs=VMEM,
            compiler_params=limit(SMALL),
            name="turn",
        )(own, *lefts)
        pieces = [*dpres] + gathered[0] + gathered[2]
        before = pl.pallas_call(
            functools.partial(sum_kernel, (0, 1, 3)),
            out_shape=jax.ShapeDtypeStruct((share, inner), F32),
            in_specs=[VMEM] * (1 + len(pieces)),
            out_specs=VMEM,
            scratch_shapes=[pltpu.VMEM((3 * rows, inner), BF16)],
            compiler_params=limit(SMALL),
            name="sum",
        )(left, *pieces)
        steps = 2
        grad = pl.pallas_call(
            functools.partial(grad_kernel, 2),
            out_shape=jax.ShapeDtypeStruct((share, inner), F32),
            in_specs=[VMEM] * (2 + len(dpres)),
            out_specs=HBM,
            scratch_shapes=[
                pltpu.VMEM((rows, inner), BF16),
                pltpu.VMEM((steps, share // steps, inner), F32),
                pltpu.SemaphoreType.DMA((steps,)),
            ],
            compiler_params=limit(SMALL),
            name="grad",
        )(left, before, *gathered[1])
        return (hidden, grad[None])
    left, right = [own], list(dpres)
    for g in range(groups):
        left += [block[:, g * share : (g + 1) * share] for block in lefts]
        right += gathered[g]
    grad = lax.dot_general(
        jnp.concatenate(left, axis=0),
        jnp.concatenate(right, axis=0),
        (((0,), (0,)), ((), ())),
        preferred_element_type=F32,
    )
    return (hidden, grad[None])


BIG, SMALL, TOUCH = 40, 12, True


def solution(mesh):
    return jax.shard_map(
        on_device,
        mesh=mesh,
        in_specs=(
            P(("dp", "expert"), None),
            P(("dp", "expert"), None),
            P(("dp", "expert")),
            P(("dp", "expert"), None),
            P("expert", None, None),
        ),
        out_specs=(P(("dp", "expert"), None), P("expert", "dp", None)),
        check_vma=False,
    )
```

```python
import functools

import jax
import jax.numpy as jnp
from jax import lax
from jax.experimental import pallas as pl
from jax.experimental.pallas import tpu as pltpu
from jax.sharding import PartitionSpec as P

LANES = 128
TAIL = 16
F32, BF16 = jnp.float32, jnp.bfloat16
HBM = pl.BlockSpec(memory_space=pltpu.HBM)
VMEM = pl.BlockSpec(memory_space=pltpu.VMEM)
ANY = pl.BlockSpec(memory_space=pl.ANY)


def limit(mebibytes):
    return pltpu.CompilerParams(vmem_limit_bytes=mebibytes << 20)


def struct(*shape):
    return jax.ShapeDtypeStruct(shape, BF16)


def swap(value, axis, offset):
    count = lax.axis_size(axis)
    return lax.ppermute(value, axis, [(i, i ^ offset) for i in range(count)])


def hold_kernel(*refs):
    pass


def after(values, *others):
    return pl.pallas_call(
        hold_kernel,
        out_shape=[jax.ShapeDtypeStruct(value.shape, value.dtype) for value in values],
        in_specs=[ANY] * (len(values) + len(others)),
        out_specs=[ANY] * len(values),
        input_output_aliases={i: i for i in range(len(values))},
        compiler_params=limit(1),
        name="hold",
    )(*values, *others)


def fetch(pairs, sems):
    copies = [pltpu.make_async_copy(a, b, sems.at[i]) for i, (a, b) in enumerate(pairs)]
    for copy in copies:
        copy.start()
    return copies


def placing_of(ids, me, step, experts, slots):
    count = ids.shape[1]
    named = lax.broadcasted_iota(jnp.int32, (experts, count), 0) == ids
    earlier = (
        lax.broadcasted_iota(jnp.int32, (count, count), 0)
        < lax.broadcasted_iota(jnp.int32, (count, count), 1)
    ).astype(BF16)
    before = jnp.dot(named.astype(BF16), earlier, preferred_element_type=F32)
    rank = jnp.sum(jnp.where(named, before, 0.0), axis=0, keepdims=True).astype(jnp.int32)
    offset = ids ^ me
    row = jnp.where(offset % step == 0, (offset // step) * slots + rank, -1)
    return lax.broadcasted_iota(jnp.int32, (experts // step * slots, count), 0) == row


def columns(ref, index, share):
    if share % LANES == 0:
        return ref[:, pl.ds(pl.multiple_of(index * share, LANES), share)]
    value = ref[...]
    total = jnp.zeros((value.shape[0], share), value.dtype)
    for g in range(value.shape[1] // share):
        total = jnp.where(index == g, value[:, g * share : (g + 1) * share], total)
    return total


def place_kernel(sizes, *refs):
    experts, slots = sizes
    hbm, outs, scratch, sems = refs[:4], refs[4:-5], refs[-5:-1], refs[-1]
    for copy in fetch(list(zip(hbm, scratch)), sems):
        copy.wait()
    outs, cuts = outs[:experts], outs[experts:]
    ids_ref, gates_ref, cots_ref, tokens_ref = scratch
    count, width = tokens_ref.shape
    inner = cots_ref.shape[1]
    names = jnp.broadcast_to(ids_ref[...].astype(F32), (TAIL, count)).astype(BF16)
    group = lax.axis_index("dp")
    for k, out in enumerate(cuts):
        share = out.shape[1]
        out[:count, :] = columns(tokens_ref, group ^ (k + 1), share)
        out[count:, :count] = names
        if share > count:
            out[count:, count:] = jnp.zeros((TAIL, share - count), BF16)
    placing = placing_of(ids_ref[...], lax.axis_index("expert"), 1, experts, slots)
    one_hot = placing.astype(BF16)
    gate = jnp.sum(jnp.where(placing, gates_ref[...].astype(F32), 0.0), axis=1, keepdims=True)
    gate = jnp.broadcast_to(gate, (gate.shape[0], LANES)).astype(BF16)
    cots = jnp.dot(one_hot, cots_ref[...], preferred_element_type=F32).astype(BF16)
    rows = jnp.dot(one_hot, tokens_ref[...], preferred_element_type=F32).astype(BF16)
    for k, out in enumerate(outs):
        here = slice(k * slots, (k + 1) * slots)
        out[:, :width] = rows[here]
        out[:, width : width + inner] = cots[here]
        out[:, width + inner :] = gate[here]


def touch_kernel(weight_ref, tie, out_ref):
    out_ref[...] = weight_ref[0, :8, :LANES]


def forward_kernel(sizes, weight_ref, *rest):
    experts, width, inner, share = sizes
    blocks, (act_ref, dpre_ref, own_ref, all_ref) = rest[:experts], rest[-4:]
    slots = blocks[0].shape[0]
    for k, block in enumerate(blocks):
        all_ref[k * slots : (k + 1) * slots, :] = block[...]
    pre = jnp.dot(all_ref[:, :width], weight_ref[0], preferred_element_type=F32)
    cots = all_ref[:, width : width + inner].astype(F32)
    gate = all_ref[:, width + inner :][:, :1].astype(F32)
    sig = jax.nn.sigmoid(pre)
    gated = gate * sig
    dpre_ref[...] = (cots * gated * (1.0 + pre * (1.0 - sig))).astype(BF16)
    act_ref[...] = (gated * pre).astype(BF16)
    own_ref[...] = columns(all_ref.at[:, :width], lax.axis_index("dp"), share)


def share_kernel(sizes, *refs):
    experts, slots, groups, count = sizes
    pairs = experts // 2
    mine, theirs, act_ref = refs[:groups], refs[groups : 2 * groups], refs[2 * groups]
    outs = refs[2 * groups + 1 :]
    share = mine[0].shape[1]
    me = lax.axis_index("expert")
    for j, out in enumerate(outs):
        out[:, groups * share :] = act_ref[2 * j * slots : 2 * (j + 1) * slots]
    for g in range(groups):
        placed = []
        for block in (mine[g], theirs[g]):
            ids = block[count:, :count][:1].astype(F32).astype(jnp.int32)
            one_hot = placing_of(ids, me, 2, experts, slots).astype(BF16)
            placed.append(
                jnp.dot(one_hot, block[:count, :], preferred_element_type=F32).astype(BF16)
            )
        for j, out in enumerate(outs):
            here = slice(j * slots, (j + 1) * slots)
            out[:, g * share : (g + 1) * share] = jnp.concatenate([p[here] for p in placed], axis=0)


def split_kernel(slots, inner, *refs):
    *blocks, out_ref = refs
    for j, block in enumerate(blocks):
        out_ref[j * slots : (j + 1) * slots] = block[slots:, block.shape[1] - inner :]


def unplace_kernel(sizes, ids_ref, theirs_ref, *refs):
    experts, slots = sizes
    *blocks, out_ref = refs
    inner = out_ref.shape[1]
    me = lax.axis_index("expert")
    mine = [block[:slots, block.shape[1] - inner :] for block in blocks]
    total = jnp.zeros(out_ref.shape, F32)
    for r, value in enumerate((jnp.concatenate(mine, axis=0), theirs_ref[...])):
        one_hot = placing_of(ids_ref[...], me ^ r, 2, experts, slots).astype(BF16)
        total = total + lax.dot_general(
            one_hot, value, (((0,), (0,)), ((), ())), preferred_element_type=F32
        )
    out_ref[...] = total.astype(BF16)


def turn_kernel(groups, own_ref, *refs):
    *blocks, out_ref = refs
    share, rows = out_ref.shape[0], own_ref.shape[0]
    out_ref[:, :rows] = own_ref[...].T
    for g in range(groups):
        value = [block[:, g * share : (g + 1) * share] for block in blocks]
        out_ref[:, (g + 1) * rows : (g + 2) * rows] = jnp.concatenate(value, axis=0).T


def sum_kernel(groups, left_ref, *refs):
    pieces, (out_ref, right_ref) = refs[:-2], refs[-2:]
    rows = left_ref.shape[1] // 4
    at = 0
    for piece in pieces:
        right_ref[at : at + piece.shape[0], :] = piece[...]
        at += piece.shape[0]
    total = jnp.zeros(out_ref.shape, F32)
    for i, g in enumerate(groups):
        total = total + jnp.dot(
            left_ref[:, g * rows : (g + 1) * rows],
            right_ref[i * rows : (i + 1) * rows, :],
            preferred_element_type=F32,
        )
    out_ref[...] = total


def grad_kernel(group, left_ref, before_ref, *refs):
    pieces, (out_hbm, right_ref, total_ref, sems) = refs[:-4], refs[-4:]
    rows = left_ref.shape[1] // 4
    at = 0
    for piece in pieces:
        right_ref[at : at + piece.shape[0], :] = piece[...]
        at += piece.shape[0]
    steps, tall = total_ref.shape[:2]
    copies = []
    for i in range(steps):
        here = slice(i * tall, (i + 1) * tall)
        total_ref[i] = before_ref[here, :] + jnp.dot(
            left_ref[here, group * rows : (group + 1) * rows],
            right_ref[...],
            preferred_element_type=F32,
        )
        copies.append(pltpu.make_async_copy(total_ref.at[i], out_hbm.at[here, :], sems.at[i]))
        copies[-1].start()
    for copy in copies:
        copy.wait()


def on_device(tokens, expert_ids, gates, cotangent, weights):
    experts, members = lax.axis_size("expert"), lax.axis_size("dp")
    group = lax.axis_index("dp")
    pairs, groups = experts // 2, members - 1
    count, width = tokens.shape
    inner = cotangent.shape[1]
    share = width // members
    slots = max(2, 2 * count // experts)
    rows = experts * slots
    wide = width + inner + LANES
    chain = slots % 16 == 0 and share % LANES == 0 and members == 4
    ids, gates = expert_ids.reshape(1, count), gates.reshape(1, count)

    mine = (ids, gates, cotangent, tokens)
    placed = pl.pallas_call(
        functools.partial(place_kernel, (experts, slots)),
        out_shape=[struct(slots, wide)] * experts + [struct(count + TAIL, share)] * groups,
        in_specs=[HBM] * 4,
        out_specs=[VMEM] * (experts + groups),
        scratch_shapes=[pltpu.VMEM(value.shape, value.dtype) for value in mine]
        + [pltpu.SemaphoreType.DMA((4,))],
        compiler_params=limit(BIG),
        name="place",
    )(*mine)
    placed, cuts = placed[:experts], placed[experts:]
    touched = pl.pallas_call(
        touch_kernel,
        out_shape=struct(8, LANES),
        in_specs=[VMEM, ANY],
        out_specs=VMEM,
        compiler_params=limit(1),
        name="touch",
    )(weights, placed[0])
    got = list(placed)
    for k in range(2, experts, 2):
        got[k] = swap(placed[k], "expert", k)
    for k in range(3, experts, 2):
        got[k] = swap(after([placed[k]], got[experts - k + 1 if k > 1 else 2], *([touched] if k == 3 else []))[0], "expert", k)
    got[1] = swap(after([placed[1]], got[2])[0], "expert", 1)
    cuts = [swap(cut, "dp", k + 1) for k, cut in enumerate(cuts)]

    act, dpre, own = pl.pallas_call(
        functools.partial(forward_kernel, (experts, width, inner, share)),
        out_shape=[struct(rows, inner), struct(rows, inner), struct(rows, share)],
        in_specs=[VMEM] * (1 + experts) + [ANY] * groups,
        out_specs=[VMEM] * 3,
        scratch_shapes=[pltpu.VMEM((rows, wide), BF16)],
        compiler_params=limit(SMALL),
        name="forward",
    )(weights, *got, *cuts)
    dpres = [dpre]

    gathered = [[] for _ in range(groups)]
    for value in dpres:
        for k in range(1, members):
            if not (chain and k == 2):
                gathered[k - 1].append(swap(value, "dp", k))
    if chain:
        ends = (group == 0) | (group == 3)
        for value, far in zip(dpres, gathered[2]):
            value = jnp.where(ends, value, far)
            gathered[1].append(lax.ppermute(value, "dp", [(0, 2), (1, 0), (2, 3), (3, 1)]))

    sent = pl.pallas_call(
        functools.partial(share_kernel, (experts, slots, groups, count)),
        out_shape=[struct(2 * slots, groups * share + inner)] * pairs,
        in_specs=[VMEM] * (1 + 2 * groups),
        out_specs=[VMEM] * pairs,
        compiler_params=limit(SMALL),
        name="place_shares",
    )(*cuts, *[swap(cut, "expert", 1) for cut in cuts], act)
    lefts = [sent[0]] + [swap(sent[j], "expert", 2 * j) for j in range(1, pairs)]
    theirs = pl.pallas_call(
        functools.partial(split_kernel, slots, inner),
        out_shape=struct(pairs * slots, inner),
        in_specs=[VMEM] * pairs,
        out_specs=VMEM,
        compiler_params=limit(SMALL),
        name="split",
    )(*lefts)
    hidden = pl.pallas_call(
        functools.partial(unplace_kernel, (experts, slots)),
        out_shape=struct(count, inner),
        in_specs=[VMEM] * (2 + pairs),
        out_specs=VMEM,
        compiler_params=limit(SMALL),
        name="unplace",
    )(ids, swap(theirs, "expert", 1), *lefts)

    if chain:
        left = pl.pallas_call(
            functools.partial(turn_kernel, groups),
            out_shape=struct(share, members * rows),
            in_specs=[VMEM] * (1 + pairs),
            out_specs=VMEM,
            compiler_params=limit(SMALL),
            name="turn",
        )(own, *lefts)
        pieces = [*dpres] + gathered[0] + gathered[2]
        before = pl.pallas_call(
            functools.partial(sum_kernel, (0, 1, 3)),
            out_shape=jax.ShapeDtypeStruct((share, inner), F32),
            in_specs=[VMEM] * (1 + len(pieces)),
            out_specs=VMEM,
            scratch_shapes=[pltpu.VMEM((3 * rows, inner), BF16)],
            compiler_params=limit(SMALL),
            name="sum",
        )(left, *pieces)
        steps = 2
        grad = pl.pallas_call(
            functools.partial(grad_kernel, 2),
            out_shape=jax.ShapeDtypeStruct((share, inner), F32),
            in_specs=[VMEM] * (2 + len(dpres)),
            out_specs=HBM,
            scratch_shapes=[
                pltpu.VMEM((rows, inner), BF16),
                pltpu.VMEM((steps, share // steps, inner), F32),
                pltpu.SemaphoreType.DMA((steps,)),
            ],
            compiler_params=limit(SMALL),
            name="grad",
        )(left, before, *gathered[1])
        return (hidden, grad[None])
    left, right = [own], list(dpres)
    for g in range(groups):
        left += [block[:, g * share : (g + 1) * share] for block in lefts]
        right += gathered[g]
    grad = lax.dot_general(
        jnp.concatenate(left, axis=0),
        jnp.concatenate(right, axis=0),
        (((0,), (0,)), ((), ())),
        preferred_element_type=F32,
    )
    return (hidden, grad[None])


BIG, SMALL, TOUCH = 40, 12, True


def solution(mesh):
    return jax.shard_map(
        on_device,
        mesh=mesh,
        in_specs=(
            P(("dp", "expert"), None),
            P(("dp", "expert"), None),
            P(("dp", "expert")),
            P(("dp", "expert"), None),
            P("expert", None, None),
        ),
        out_specs=(P(("dp", "expert"), None), P("expert", "dp", None)),
        check_vma=False,
    )
```

```python
import functools

import jax
import jax.numpy as jnp
from jax import lax
from jax.experimental import pallas as pl
from jax.experimental.pallas import tpu as pltpu
from jax.sharding import PartitionSpec as P

LANES = 128
TAIL = 16
F32, BF16 = jnp.float32, jnp.bfloat16
HBM = pl.BlockSpec(memory_space=pltpu.HBM)
VMEM = pl.BlockSpec(memory_space=pltpu.VMEM)
ANY = pl.BlockSpec(memory_space=pl.ANY)


def limit(mebibytes):
    return pltpu.CompilerParams(vmem_limit_bytes=mebibytes << 20)


def struct(*shape):
    return jax.ShapeDtypeStruct(shape, BF16)


def swap(value, axis, offset):
    count = lax.axis_size(axis)
    return lax.ppermute(value, axis, [(i, i ^ offset) for i in range(count)])


def hold_kernel(*refs):
    pass


def after(values, *others):
    return pl.pallas_call(
        hold_kernel,
        out_shape=[jax.ShapeDtypeStruct(value.shape, value.dtype) for value in values],
        in_specs=[ANY] * (len(values) + len(others)),
        out_specs=[ANY] * len(values),
        input_output_aliases={i: i for i in range(len(values))},
        compiler_params=limit(1),
        name="hold",
    )(*values, *others)


def fetch(pairs, sems):
    copies = [pltpu.make_async_copy(a, b, sems.at[i]) for i, (a, b) in enumerate(pairs)]
    for copy in copies:
        copy.start()
    return copies


def placing_of(ids, me, step, experts, slots):
    count = ids.shape[1]
    named = lax.broadcasted_iota(jnp.int32, (experts, count), 0) == ids
    earlier = (
        lax.broadcasted_iota(jnp.int32, (count, count), 0)
        < lax.broadcasted_iota(jnp.int32, (count, count), 1)
    ).astype(BF16)
    before = jnp.dot(named.astype(BF16), earlier, preferred_element_type=F32)
    rank = jnp.sum(jnp.where(named, before, 0.0), axis=0, keepdims=True).astype(jnp.int32)
    offset = ids ^ me
    row = jnp.where(offset % step == 0, (offset // step) * slots + rank, -1)
    return lax.broadcasted_iota(jnp.int32, (experts // step * slots, count), 0) == row


def columns(ref, index, share):
    if share % LANES == 0:
        return ref[:, pl.ds(pl.multiple_of(index * share, LANES), share)]
    value = ref[...]
    total = jnp.zeros((value.shape[0], share), value.dtype)
    for g in range(value.shape[1] // share):
        total = jnp.where(index == g, value[:, g * share : (g + 1) * share], total)
    return total


def place_kernel(sizes, *refs):
    experts, slots = sizes
    hbm, outs, scratch, sems = refs[:4], refs[4:-5], refs[-5:-1], refs[-1]
    for copy in fetch(list(zip(hbm, scratch)), sems):
        copy.wait()
    outs, cuts = outs[:experts], outs[experts:]
    ids_ref, gates_ref, cots_ref, tokens_ref = scratch
    count, width = tokens_ref.shape
    inner = cots_ref.shape[1]
    names = jnp.broadcast_to(ids_ref[...].astype(F32), (TAIL, count)).astype(BF16)
    group = lax.axis_index("dp")
    for k, out in enumerate(cuts):
        share = out.shape[1]
        out[:count, :] = columns(tokens_ref, group ^ (k + 1), share)
        out[count:, :count] = names
        if share > count:
            out[count:, count:] = jnp.zeros((TAIL, share - count), BF16)
    placing = placing_of(ids_ref[...], lax.axis_index("expert"), 1, experts, slots)
    one_hot = placing.astype(BF16)
    gate = jnp.sum(jnp.where(placing, gates_ref[...].astype(F32), 0.0), axis=1, keepdims=True)
    gate = jnp.broadcast_to(gate, (gate.shape[0], LANES)).astype(BF16)
    cots = jnp.dot(one_hot, cots_ref[...], preferred_element_type=F32).astype(BF16)
    rows = jnp.dot(one_hot, tokens_ref[...], preferred_element_type=F32).astype(BF16)
    for k, out in enumerate(outs):
        here = slice(k * slots, (k + 1) * slots)
        out[:, :width] = rows[here]
        out[:, width : width + inner] = cots[here]
        out[:, width + inner :] = gate[here]


def touch_kernel(weight_ref, tie, out_ref):
    out_ref[...] = weight_ref[0, :8, :LANES]


def forward_kernel(sizes, weight_ref, *rest):
    count, width, inner, share = sizes
    blocks, (act_ref, dpre_ref, own_ref, all_ref) = rest[:count], rest[-4:]
    joined = dpre_ref.shape[0] - all_ref.shape[0]
    if joined:
        dpre_ref[:joined, :] = rest[count][...]
    slots = blocks[0].shape[0]
    for k, block in enumerate(blocks):
        all_ref[k * slots : (k + 1) * slots, :] = block[...]
    pre = jnp.dot(all_ref[:, :width], weight_ref[0], preferred_element_type=F32)
    cots = all_ref[:, width : width + inner].astype(F32)
    gate = all_ref[:, width + inner :][:, :1].astype(F32)
    sig = jax.nn.sigmoid(pre)
    gated = gate * sig
    dpre_ref[joined:, :] = (cots * gated * (1.0 + pre * (1.0 - sig))).astype(BF16)
    act_ref[...] = (gated * pre).astype(BF16)
    own_ref[...] = columns(all_ref.at[:, :width], lax.axis_index("dp"), share)


def share_kernel(sizes, *refs):
    experts, slots, groups, count = sizes
    pairs = experts // 2
    mine, theirs, acts = refs[:groups], refs[groups : 2 * groups], refs[2 * groups : 2 * groups + 2]
    outs = refs[2 * groups + 2 :]
    share = mine[0].shape[1]
    me = lax.axis_index("expert")
    for j, out in enumerate(outs):
        for r in range(2):
            here = slice(j * slots, (j + 1) * slots)
            out[r * slots : (r + 1) * slots, groups * share :] = acts[r][here]
    for g in range(groups):
        placed = []
        for block in (mine[g], theirs[g]):
            ids = block[count:, :count][:1].astype(F32).astype(jnp.int32)
            one_hot = placing_of(ids, me, 2, experts, slots).astype(BF16)
            placed.append(
                jnp.dot(one_hot, block[:count, :], preferred_element_type=F32).astype(BF16)
            )
        for j, out in enumerate(outs):
            here = slice(j * slots, (j + 1) * slots)
            out[:, g * share : (g + 1) * share] = jnp.concatenate([p[here] for p in placed], axis=0)


def split_kernel(slots, inner, *refs):
    *blocks, out_ref = refs
    for j, block in enumerate(blocks):
        out_ref[j * slots : (j + 1) * slots] = block[slots:, block.shape[1] - inner :]


def unplace_kernel(sizes, ids_ref, theirs_ref, *refs):
    experts, slots = sizes
    *blocks, out_ref = refs
    inner = out_ref.shape[1]
    me = lax.axis_index("expert")
    mine = [block[:slots, block.shape[1] - inner :] for block in blocks]
    total = jnp.zeros(out_ref.shape, F32)
    for r, value in enumerate((jnp.concatenate(mine, axis=0), theirs_ref[...])):
        one_hot = placing_of(ids_ref[...], me ^ r, 2, experts, slots).astype(BF16)
        total = total + lax.dot_general(
            one_hot, value, (((0,), (0,)), ((), ())), preferred_element_type=F32
        )
    out_ref[...] = total.astype(BF16)


def turn_kernel(groups, *refs):
    own, blocks, out_ref = refs[:2], refs[2:-1], refs[-1]
    share, rows = out_ref.shape[0], own[0].shape[0]
    slots = blocks[0].shape[0] // 2
    for r in range(2):
        out_ref[:, r * rows : (r + 1) * rows] = own[r][...].T
        for g in range(groups):
            value = [block[r * slots : (r + 1) * slots, g * share : (g + 1) * share] for block in blocks]
            at = (2 * g + 2 + r) * rows
            out_ref[:, at : at + rows] = jnp.concatenate(value, axis=0).T


def sum_kernel(groups, left_ref, *refs):
    pieces, (out_ref, right_ref) = refs[:-2], refs[-2:]
    rows = left_ref.shape[1] // 4
    at = 0
    for piece in pieces:
        right_ref[at : at + piece.shape[0], :] = piece[...]
        at += piece.shape[0]
    total = jnp.zeros(out_ref.shape, F32)
    for i, g in enumerate(groups):
        total = total + jnp.dot(
            left_ref[:, g * rows : (g + 1) * rows],
            right_ref[i * rows : (i + 1) * rows, :],
            preferred_element_type=F32,
        )
    out_ref[...] = total


def grad_kernel(group, left_ref, before_ref, *refs):
    pieces, (out_hbm, right_ref, total_ref, sems) = refs[:-4], refs[-4:]
    rows = left_ref.shape[1] // 4
    at = 0
    for piece in pieces:
        right_ref[at : at + piece.shape[0], :] = piece[...]
        at += piece.shape[0]
    steps, tall = total_ref.shape[:2]
    copies = []
    for i in range(steps):
        here = slice(i * tall, (i + 1) * tall)
        total_ref[i] = before_ref[here, :] + jnp.dot(
            left_ref[here, group * rows : (group + 1) * rows],
            right_ref[...],
            preferred_element_type=F32,
        )
        copies.append(pltpu.make_async_copy(total_ref.at[i], out_hbm.at[here, :], sems.at[i]))
        copies[-1].start()
    for copy in copies:
        copy.wait()


def on_device(tokens, expert_ids, gates, cotangent, weights):
    experts, members = lax.axis_size("expert"), lax.axis_size("dp")
    group = lax.axis_index("dp")
    pairs, groups = experts // 2, members - 1
    count, width = tokens.shape
    inner = cotangent.shape[1]
    share = width // members
    slots = max(2, 2 * count // experts)
    rows = experts * slots
    wide = width + inner + LANES
    chain = slots % 16 == 0 and share % LANES == 0 and members == 4
    ids, gates = expert_ids.reshape(1, count), gates.reshape(1, count)

    mine = (ids, gates, cotangent, tokens)
    placed = pl.pallas_call(
        functools.partial(place_kernel, (experts, slots)),
        out_shape=[struct(slots, wide)] * experts + [struct(count + TAIL, share)] * groups,
        in_specs=[HBM] * 4,
        out_specs=[VMEM] * (experts + groups),
        scratch_shapes=[pltpu.VMEM(value.shape, value.dtype) for value in mine]
        + [pltpu.SemaphoreType.DMA((4,))],
        compiler_params=limit(BIG),
        name="place",
    )(*mine)
    placed, cuts = placed[:experts], placed[experts:]
    touched = pl.pallas_call(
        touch_kernel,
        out_shape=struct(8, LANES),
        in_specs=[VMEM, ANY],
        out_specs=VMEM,
        compiler_params=limit(1),
        name="touch",
    )(weights, placed[0])
    got = list(placed)
    for k in range(2, experts, 2):
        got[k] = swap(placed[k], "expert", k)
    for k in range(3, experts, 2):
        got[k] = swap(after([placed[k]], got[experts - k + 1 if k > 1 else 2], *([touched] if k == 3 else []))[0], "expert", k)
    got[1] = swap(after([placed[1]], got[2])[0], "expert", 1)
    cuts = [swap(cut, "dp", k + 1) for k, cut in enumerate(cuts)]

    def forward(blocks, before, *ties):
        height = len(blocks) * slots
        joined = height + sum(value.shape[0] for value in before)
        return pl.pallas_call(
            functools.partial(forward_kernel, (len(blocks), width, inner, share)),
            out_shape=[struct(height, inner), struct(joined, inner), struct(height, share)],
            in_specs=[VMEM] * (1 + len(blocks) + len(before)) + [ANY] * len(ties),
            out_specs=[VMEM] * 3,
            scratch_shapes=[pltpu.VMEM((height, wide), BF16)],
            compiler_params=limit(SMALL),
            name="forward",
        )(weights, *blocks, *before, *ties)

    act, half, own = forward(got[::2], [], cuts[0])
    acts, owns = [act], [own]
    early = [swap(half, "dp", 3)] if chain else []
    crossed = [swap(cut, "expert", 1) for cut in cuts]
    act, dpre, own = forward(got[1::2], [half], *cuts, crossed[0])
    acts, owns, dpres = acts + [act], owns + [own], [dpre]
    gathered = [[] for _ in range(groups)]
    for k in range(1, members):
        if chain and k == 3:
            gathered[2] = [*early, swap(dpre[rows // 2 :], "dp", 3)]
        elif not (chain and k == 2):
            gathered[k - 1].append(swap(dpre, "dp", k))
    if chain:
        ends = (group == 0) | (group == 3)
        value = jnp.where(ends, dpre, jnp.concatenate(gathered[2], axis=0))
        gathered[1].append(lax.ppermute(value, "dp", [(0, 2), (1, 0), (2, 3), (3, 1)]))

    sent = pl.pallas_call(
        functools.partial(share_kernel, (experts, slots, groups, count)),
        out_shape=[struct(2 * slots, groups * share + inner)] * pairs,
        in_specs=[VMEM] * (2 + 2 * groups),
        out_specs=[VMEM] * pairs,
        compiler_params=limit(SMALL),
        name="place_shares",
    )(*cuts, *crossed, *acts)
    lefts = [sent[0]] + [swap(sent[j], "expert", 2 * j) for j in range(1, pairs)]
    theirs = pl.pallas_call(
        functools.partial(split_kernel, slots, inner),
        out_shape=struct(pairs * slots, inner),
        in_specs=[VMEM] * pairs,
        out_specs=VMEM,
        compiler_params=limit(SMALL),
        name="split",
    )(*lefts)
    hidden = pl.pallas_call(
        functools.partial(unplace_kernel, (experts, slots)),
        out_shape=struct(count, inner),
        in_specs=[VMEM] * (2 + pairs),
        out_specs=VMEM,
        compiler_params=limit(SMALL),
        name="unplace",
    )(ids, swap(theirs, "expert", 1), *lefts)

    if chain:
        left = pl.pallas_call(
            functools.partial(turn_kernel, groups),
            out_shape=struct(share, members * rows),
            in_specs=[VMEM] * (2 + pairs),
            out_specs=VMEM,
            compiler_params=limit(SMALL),
            name="turn",
        )(*owns, *lefts)
        pieces = [*dpres] + gathered[0] + gathered[2]
        before = pl.pallas_call(
            functools.partial(sum_kernel, (0, 1, 3)),
            out_shape=jax.ShapeDtypeStruct((share, inner), F32),
            in_specs=[VMEM] * (1 + len(pieces)),
            out_specs=VMEM,
            scratch_shapes=[pltpu.VMEM((3 * rows, inner), BF16)],
            compiler_params=limit(SMALL),
            name="sum",
        )(left, *pieces)
        steps = 2
        grad = pl.pallas_call(
            functools.partial(grad_kernel, 2),
            out_shape=jax.ShapeDtypeStruct((share, inner), F32),
            in_specs=[VMEM] * (2 + len(dpres)),
            out_specs=HBM,
            scratch_shapes=[
                pltpu.VMEM((rows, inner), BF16),
                pltpu.VMEM((steps, share // steps, inner), F32),
                pltpu.SemaphoreType.DMA((steps,)),
            ],
            compiler_params=limit(SMALL),
            name="grad",
        )(left, before, *gathered[1])
        return (hidden, grad[None])
    left, right = list(owns), list(dpres)
    for g in range(groups):
        here = slice(g * share, (g + 1) * share)
        left += [b[r * slots : (r + 1) * slots, here] for r in range(2) for b in lefts]
        right += gathered[g]
    grad = lax.dot_general(
        jnp.concatenate(left, axis=0),
        jnp.concatenate(right, axis=0),
        (((0,), (0,)), ((), ())),
        preferred_element_type=F32,
    )
    return (hidden, grad[None])


BIG, SMALL, TOUCH, TIES = 40, 12, True, 1


def solution(mesh):
    return jax.shard_map(
        on_device,
        mesh=mesh,
        in_specs=(
            P(("dp", "expert"), None),
            P(("dp", "expert"), None),
            P(("dp", "expert")),
            P(("dp", "expert"), None),
            P("expert", None, None),
        ),
        out_specs=(P(("dp", "expert"), None), P("expert", "dp", None)),
        check_vma=False,
    )
```

```python
import functools

import jax
import jax.numpy as jnp
from jax import lax
from jax.experimental import pallas as pl
from jax.experimental.pallas import tpu as pltpu
from jax.sharding import PartitionSpec as P

LANES = 128
TAIL = 16
F32, BF16 = jnp.float32, jnp.bfloat16
HBM = pl.BlockSpec(memory_space=pltpu.HBM)
VMEM = pl.BlockSpec(memory_space=pltpu.VMEM)
ANY = pl.BlockSpec(memory_space=pl.ANY)


def limit(mebibytes):
    return pltpu.CompilerParams(vmem_limit_bytes=mebibytes << 20)


def struct(*shape):
    return jax.ShapeDtypeStruct(shape, BF16)


def swap(value, axis, offset):
    count = lax.axis_size(axis)
    return lax.ppermute(value, axis, [(i, i ^ offset) for i in range(count)])


def hold_kernel(*refs):
    pass


def after(values, *others):
    return pl.pallas_call(
        hold_kernel,
        out_shape=[jax.ShapeDtypeStruct(value.shape, value.dtype) for value in values],
        in_specs=[ANY] * (len(values) + len(others)),
        out_specs=[ANY] * len(values),
        input_output_aliases={i: i for i in range(len(values))},
        compiler_params=limit(1),
        name="hold",
    )(*values, *others)


def fetch(pairs, sems):
    copies = [pltpu.make_async_copy(a, b, sems.at[i]) for i, (a, b) in enumerate(pairs)]
    for copy in copies:
        copy.start()
    return copies


def placing_of(ids, me, step, experts, slots):
    count = ids.shape[1]
    named = lax.broadcasted_iota(jnp.int32, (experts, count), 0) == ids
    earlier = (
        lax.broadcasted_iota(jnp.int32, (count, count), 0)
        < lax.broadcasted_iota(jnp.int32, (count, count), 1)
    ).astype(BF16)
    before = jnp.dot(named.astype(BF16), earlier, preferred_element_type=F32)
    rank = jnp.sum(jnp.where(named, before, 0.0), axis=0, keepdims=True).astype(jnp.int32)
    offset = ids ^ me
    row = jnp.where(offset % step == 0, (offset // step) * slots + rank, -1)
    return lax.broadcasted_iota(jnp.int32, (experts // step * slots, count), 0) == row


def columns(ref, index, share):
    if share % LANES == 0:
        return ref[:, pl.ds(pl.multiple_of(index * share, LANES), share)]
    value = ref[...]
    total = jnp.zeros((value.shape[0], share), value.dtype)
    for g in range(value.shape[1] // share):
        total = jnp.where(index == g, value[:, g * share : (g + 1) * share], total)
    return total


def place_kernel(sizes, *refs):
    experts, slots = sizes
    hbm, outs, scratch, sems = refs[:4], refs[4:-5], refs[-5:-1], refs[-1]
    for copy in fetch(list(zip(hbm, scratch)), sems):
        copy.wait()
    outs, cuts = outs[:experts], outs[experts:]
    ids_ref, gates_ref, cots_ref, tokens_ref = scratch
    count, width = tokens_ref.shape
    inner = cots_ref.shape[1]
    names = jnp.broadcast_to(ids_ref[...].astype(F32), (TAIL, count)).astype(BF16)
    group = lax.axis_index("dp")
    for k, out in enumerate(cuts):
        share = out.shape[1]
        out[:count, :] = columns(tokens_ref, group ^ (k + 1), share)
        out[count:, :count] = names
        if share > count:
            out[count:, count:] = jnp.zeros((TAIL, share - count), BF16)
    placing = placing_of(ids_ref[...], lax.axis_index("expert"), 1, experts, slots)
    one_hot = placing.astype(BF16)
    gate = jnp.sum(jnp.where(placing, gates_ref[...].astype(F32), 0.0), axis=1, keepdims=True)
    gate = jnp.broadcast_to(gate, (gate.shape[0], LANES)).astype(BF16)
    cots = jnp.dot(one_hot, cots_ref[...], preferred_element_type=F32).astype(BF16)
    rows = jnp.dot(one_hot, tokens_ref[...], preferred_element_type=F32).astype(BF16)
    for k, out in enumerate(outs):
        here = slice(k * slots, (k + 1) * slots)
        out[:, :width] = rows[here]
        out[:, width : width + inner] = cots[here]
        out[:, width + inner :] = gate[here]


def touch_kernel(weight_ref, tie, out_ref):
    out_ref[...] = weight_ref[0, :8, :LANES]


def forward_kernel(sizes, weight_ref, *rest):
    count, width, inner, share = sizes
    blocks, (act_ref, dpre_ref, own_ref, all_ref) = rest[:count], rest[-4:]
    joined = dpre_ref.shape[0] - all_ref.shape[0]
    if joined:
        dpre_ref[:joined, :] = rest[count][...]
    slots = blocks[0].shape[0]
    for k, block in enumerate(blocks):
        all_ref[k * slots : (k + 1) * slots, :] = block[...]
    pre = jnp.dot(all_ref[:, :width], weight_ref[0], preferred_element_type=F32)
    cots = all_ref[:, width : width + inner].astype(F32)
    gate = all_ref[:, width + inner :][:, :1].astype(F32)
    sig = jax.nn.sigmoid(pre)
    gated = gate * sig
    dpre_ref[joined:, :] = (cots * gated * (1.0 + pre * (1.0 - sig))).astype(BF16)
    act_ref[...] = (gated * pre).astype(BF16)
    own_ref[...] = columns(all_ref.at[:, :width], lax.axis_index("dp"), share)


def share_kernel(sizes, *refs):
    experts, slots, groups, count = sizes
    pairs = experts // 2
    mine, theirs, acts = refs[:groups], refs[groups : 2 * groups], refs[2 * groups : 2 * groups + 2]
    outs = refs[2 * groups + 2 :]
    share = mine[0].shape[1]
    me = lax.axis_index("expert")
    for j, out in enumerate(outs):
        for r in range(2):
            here = slice(j * slots, (j + 1) * slots)
            out[r * slots : (r + 1) * slots, groups * share :] = acts[r][here]
    for g in range(groups):
        placed = []
        for block in (mine[g], theirs[g]):
            ids = block[count:, :count][:1].astype(F32).astype(jnp.int32)
            one_hot = placing_of(ids, me, 2, experts, slots).astype(BF16)
            placed.append(
                jnp.dot(one_hot, block[:count, :], preferred_element_type=F32).astype(BF16)
            )
        for j, out in enumerate(outs):
            here = slice(j * slots, (j + 1) * slots)
            out[:, g * share : (g + 1) * share] = jnp.concatenate([p[here] for p in placed], axis=0)


def split_kernel(slots, inner, *refs):
    *blocks, out_ref = refs
    for j, block in enumerate(blocks):
        out_ref[j * slots : (j + 1) * slots] = block[slots:, block.shape[1] - inner :]


def unplace_kernel(sizes, ids_ref, theirs_ref, *refs):
    experts, slots = sizes
    *blocks, out_ref = refs
    inner = out_ref.shape[1]
    me = lax.axis_index("expert")
    mine = [block[:slots, block.shape[1] - inner :] for block in blocks]
    total = jnp.zeros(out_ref.shape, F32)
    for r, value in enumerate((jnp.concatenate(mine, axis=0), theirs_ref[...])):
        one_hot = placing_of(ids_ref[...], me ^ r, 2, experts, slots).astype(BF16)
        total = total + lax.dot_general(
            one_hot, value, (((0,), (0,)), ((), ())), preferred_element_type=F32
        )
    out_ref[...] = total.astype(BF16)


def turn_kernel(groups, *refs):
    own, blocks, out_ref = refs[:2], refs[2:-1], refs[-1]
    share, rows = out_ref.shape[0], own[0].shape[0]
    slots = blocks[0].shape[0] // 2
    for r in range(2):
        out_ref[:, r * rows : (r + 1) * rows] = own[r][...].T
        for g in range(groups):
            value = [block[r * slots : (r + 1) * slots, g * share : (g + 1) * share] for block in blocks]
            at = (2 * g + 2 + r) * rows
            out_ref[:, at : at + rows] = jnp.concatenate(value, axis=0).T


def sum_kernel(groups, left_ref, *refs):
    pieces, (out_ref, right_ref) = refs[:-2], refs[-2:]
    rows = left_ref.shape[1] // 4
    at = 0
    for piece in pieces:
        right_ref[at : at + piece.shape[0], :] = piece[...]
        at += piece.shape[0]
    total = jnp.zeros(out_ref.shape, F32)
    for i, g in enumerate(groups):
        total = total + jnp.dot(
            left_ref[:, g * rows : (g + 1) * rows],
            right_ref[i * rows : (i + 1) * rows, :],
            preferred_element_type=F32,
        )
    out_ref[...] = total


def grad_kernel(group, left_ref, before_ref, *refs):
    pieces, (out_hbm, right_ref, total_ref, sems) = refs[:-4], refs[-4:]
    rows = left_ref.shape[1] // 4
    at = 0
    for piece in pieces:
        right_ref[at : at + piece.shape[0], :] = piece[...]
        at += piece.shape[0]
    steps, tall = total_ref.shape[:2]
    copies = []
    for i in range(steps):
        here = slice(i * tall, (i + 1) * tall)
        total_ref[i] = before_ref[here, :] + jnp.dot(
            left_ref[here, group * rows : (group + 1) * rows],
            right_ref[...],
            preferred_element_type=F32,
        )
        copies.append(pltpu.make_async_copy(total_ref.at[i], out_hbm.at[here, :], sems.at[i]))
        copies[-1].start()
    for copy in copies:
        copy.wait()


def on_device(tokens, expert_ids, gates, cotangent, weights):
    experts, members = lax.axis_size("expert"), lax.axis_size("dp")
    group = lax.axis_index("dp")
    pairs, groups = experts // 2, members - 1
    count, width = tokens.shape
    inner = cotangent.shape[1]
    share = width // members
    slots = max(2, 2 * count // experts)
    rows = experts * slots
    wide = width + inner + LANES
    chain = slots % 16 == 0 and share % LANES == 0 and members == 4
    ids, gates = expert_ids.reshape(1, count), gates.reshape(1, count)

    mine = (ids, gates, cotangent, tokens)
    placed = pl.pallas_call(
        functools.partial(place_kernel, (experts, slots)),
        out_shape=[struct(slots, wide)] * experts + [struct(count + TAIL, share)] * groups,
        in_specs=[HBM] * 4,
        out_specs=[VMEM] * (experts + groups),
        scratch_shapes=[pltpu.VMEM(value.shape, value.dtype) for value in mine]
        + [pltpu.SemaphoreType.DMA((4,))],
        compiler_params=limit(BIG),
        name="place",
    )(*mine)
    placed, cuts = placed[:experts], placed[experts:]
    touched = pl.pallas_call(
        touch_kernel,
        out_shape=struct(8, LANES),
        in_specs=[VMEM, ANY],
        out_specs=VMEM,
        compiler_params=limit(1),
        name="touch",
    )(weights, placed[0])
    got = list(placed)
    for k in range(2, experts, 2):
        got[k] = swap(placed[k], "expert", k)
    for k in range(3, experts, 2):
        got[k] = swap(after([placed[k]], got[experts - k + 1 if k > 1 else 2], *([touched] if k == 3 else []))[0], "expert", k)
    got[1] = swap(after([placed[1]], got[2])[0], "expert", 1)
    cuts = [swap(cut, "dp", k + 1) for k, cut in enumerate(cuts)]

    def forward(blocks, before, *ties):
        height = len(blocks) * slots
        joined = height + sum(value.shape[0] for value in before)
        return pl.pallas_call(
            functools.partial(forward_kernel, (len(blocks), width, inner, share)),
            out_shape=[struct(height, inner), struct(joined, inner), struct(height, share)],
            in_specs=[VMEM] * (1 + len(blocks) + len(before)) + [ANY] * len(ties),
            out_specs=[VMEM] * 3,
            scratch_shapes=[pltpu.VMEM((height, wide), BF16)],
            compiler_params=limit(SMALL),
            name="forward",
        )(weights, *blocks, *before, *ties)

    act, half, own = forward(got[::2], [], cuts[0])
    acts, owns = [act], [own]
    early = [swap(half, "dp", 3)] if chain else []
    crossed = [swap(cut, "expert", 1) for cut in cuts]
    act, dpre, own = forward(got[1::2], [half], *cuts, crossed[0])
    acts, owns, dpres = acts + [act], owns + [own], [dpre]
    gathered = [[] for _ in range(groups)]
    for k in reversed(range(1, members)):
        if chain and k == 3:
            gathered[2] = [*early, swap(dpre[rows // 2 :], "dp", 3)]
        elif not (chain and k == 2):
            gathered[k - 1].append(swap(dpre, "dp", k))
    if chain:
        ends = (group == 0) | (group == 3)
        value = jnp.where(ends, dpre, jnp.concatenate(gathered[2], axis=0))
        gathered[1].append(lax.ppermute(value, "dp", [(0, 2), (1, 0), (2, 3), (3, 1)]))

    sent = pl.pallas_call(
        functools.partial(share_kernel, (experts, slots, groups, count)),
        out_shape=[struct(2 * slots, groups * share + inner)] * pairs,
        in_specs=[VMEM] * (2 + 2 * groups),
        out_specs=[VMEM] * pairs,
        compiler_params=limit(SMALL),
        name="place_shares",
    )(*cuts, *crossed, *acts)
    lefts = [sent[0]] + [swap(sent[j], "expert", 2 * j) for j in range(1, pairs)]
    theirs = pl.pallas_call(
        functools.partial(split_kernel, slots, inner),
        out_shape=struct(pairs * slots, inner),
        in_specs=[VMEM] * pairs,
        out_specs=VMEM,
        compiler_params=limit(SMALL),
        name="split",
    )(*lefts)
    hidden = pl.pallas_call(
        functools.partial(unplace_kernel, (experts, slots)),
        out_shape=struct(count, inner),
        in_specs=[VMEM] * (2 + pairs),
        out_specs=VMEM,
        compiler_params=limit(SMALL),
        name="unplace",
    )(ids, swap(theirs, "expert", 1), *lefts)

    if chain:
        left = pl.pallas_call(
            functools.partial(turn_kernel, groups),
            out_shape=struct(share, members * rows),
            in_specs=[VMEM] * (2 + pairs),
            out_specs=VMEM,
            compiler_params=limit(SMALL),
            name="turn",
        )(*owns, *lefts)
        pieces = [*dpres] + gathered[0] + gathered[2]
        before = pl.pallas_call(
            functools.partial(sum_kernel, (0, 1, 3)),
            out_shape=jax.ShapeDtypeStruct((share, inner), F32),
            in_specs=[VMEM] * (1 + len(pieces)),
            out_specs=VMEM,
            scratch_shapes=[pltpu.VMEM((3 * rows, inner), BF16)],
            compiler_params=limit(SMALL),
            name="sum",
        )(left, *pieces)
        steps = 2
        grad = pl.pallas_call(
            functools.partial(grad_kernel, 2),
            out_shape=jax.ShapeDtypeStruct((share, inner), F32),
            in_specs=[VMEM] * (2 + len(dpres)),
            out_specs=HBM,
            scratch_shapes=[
                pltpu.VMEM((rows, inner), BF16),
                pltpu.VMEM((steps, share // steps, inner), F32),
                pltpu.SemaphoreType.DMA((steps,)),
            ],
            compiler_params=limit(SMALL),
            name="grad",
        )(left, before, *gathered[1])
        return (hidden, grad[None])
    left, right = list(owns), list(dpres)
    for g in range(groups):
        here = slice(g * share, (g + 1) * share)
        left += [b[r * slots : (r + 1) * slots, here] for r in range(2) for b in lefts]
        right += gathered[g]
    grad = lax.dot_general(
        jnp.concatenate(left, axis=0),
        jnp.concatenate(right, axis=0),
        (((0,), (0,)), ((), ())),
        preferred_element_type=F32,
    )
    return (hidden, grad[None])


BIG, SMALL, TOUCH, TIES = 40, 12, True, 1


def solution(mesh):
    return jax.shard_map(
        on_device,
        mesh=mesh,
        in_specs=(
            P(("dp", "expert"), None),
            P(("dp", "expert"), None),
            P(("dp", "expert")),
            P(("dp", "expert"), None),
            P("expert", None, None),
        ),
        out_specs=(P(("dp", "expert"), None), P("expert", "dp", None)),
        check_vma=False,
    )
```

```python
import functools

import jax
import jax.numpy as jnp
from jax import lax
from jax.experimental import pallas as pl
from jax.experimental.pallas import tpu as pltpu
from jax.sharding import PartitionSpec as P

LANES = 128
TAIL = 16
F32, BF16 = jnp.float32, jnp.bfloat16
HBM = pl.BlockSpec(memory_space=pltpu.HBM)
VMEM = pl.BlockSpec(memory_space=pltpu.VMEM)
ANY = pl.BlockSpec(memory_space=pl.ANY)


def limit(mebibytes):
    return pltpu.CompilerParams(vmem_limit_bytes=mebibytes << 20)


def struct(*shape):
    return jax.ShapeDtypeStruct(shape, BF16)


def swap(value, axis, offset):
    count = lax.axis_size(axis)
    return lax.ppermute(value, axis, [(i, i ^ offset) for i in range(count)])


def hold_kernel(*refs):
    pass


def after(values, *others):
    return pl.pallas_call(
        hold_kernel,
        out_shape=[jax.ShapeDtypeStruct(value.shape, value.dtype) for value in values],
        in_specs=[ANY] * (len(values) + len(others)),
        out_specs=[ANY] * len(values),
        input_output_aliases={i: i for i in range(len(values))},
        compiler_params=limit(1),
        name="hold",
    )(*values, *others)


def fetch(pairs, sems):
    copies = [pltpu.make_async_copy(a, b, sems.at[i]) for i, (a, b) in enumerate(pairs)]
    for copy in copies:
        copy.start()
    return copies


def placing_of(ids, me, step, experts, slots):
    count = ids.shape[1]
    named = lax.broadcasted_iota(jnp.int32, (experts, count), 0) == ids
    earlier = (
        lax.broadcasted_iota(jnp.int32, (count, count), 0)
        < lax.broadcasted_iota(jnp.int32, (count, count), 1)
    ).astype(BF16)
    before = jnp.dot(named.astype(BF16), earlier, preferred_element_type=F32)
    rank = jnp.sum(jnp.where(named, before, 0.0), axis=0, keepdims=True).astype(jnp.int32)
    offset = ids ^ me
    row = jnp.where(offset % step == 0, (offset // step) * slots + rank, -1)
    return lax.broadcasted_iota(jnp.int32, (experts // step * slots, count), 0) == row


def columns(ref, index, share):
    if share % LANES == 0:
        return ref[:, pl.ds(pl.multiple_of(index * share, LANES), share)]
    value = ref[...]
    total = jnp.zeros((value.shape[0], share), value.dtype)
    for g in range(value.shape[1] // share):
        total = jnp.where(index == g, value[:, g * share : (g + 1) * share], total)
    return total


def place_kernel(sizes, *refs):
    experts, slots = sizes
    hbm, outs, scratch, sems = refs[:4], refs[4:-5], refs[-5:-1], refs[-1]
    for copy in fetch(list(zip(hbm, scratch)), sems):
        copy.wait()
    outs, cuts = outs[:experts], outs[experts:]
    ids_ref, gates_ref, cots_ref, tokens_ref = scratch
    count, width = tokens_ref.shape
    inner = cots_ref.shape[1]
    names = jnp.broadcast_to(ids_ref[...].astype(F32), (TAIL, count)).astype(BF16)
    group = lax.axis_index("dp")
    for k, out in enumerate(cuts):
        share = out.shape[1]
        out[:count, :] = columns(tokens_ref, group ^ (k + 1), share)
        out[count:, :count] = names
        if share > count:
            out[count:, count:] = jnp.zeros((TAIL, share - count), BF16)
    placing = placing_of(ids_ref[...], lax.axis_index("expert"), 1, experts, slots)
    one_hot = placing.astype(BF16)
    gate = jnp.sum(jnp.where(placing, gates_ref[...].astype(F32), 0.0), axis=1, keepdims=True)
    gate = jnp.broadcast_to(gate, (gate.shape[0], LANES)).astype(BF16)
    cots = jnp.dot(one_hot, cots_ref[...], preferred_element_type=F32).astype(BF16)
    rows = jnp.dot(one_hot, tokens_ref[...], preferred_element_type=F32).astype(BF16)
    for k, out in enumerate(outs):
        here = slice(k * slots, (k + 1) * slots)
        out[:, :width] = rows[here]
        out[:, width : width + inner] = cots[here]
        out[:, width + inner :] = gate[here]


def touch_kernel(weight_ref, tie, out_ref):
    out_ref[...] = weight_ref[0, :8, :LANES]


def forward_kernel(sizes, weight_ref, *rest):
    count, width, inner, share = sizes
    blocks, (act_ref, dpre_ref, own_ref, all_ref) = rest[:count], rest[-4:]
    joined = dpre_ref.shape[0] - all_ref.shape[0]
    if joined:
        dpre_ref[:joined, :] = rest[count][...]
    slots = blocks[0].shape[0]
    for k, block in enumerate(blocks):
        all_ref[k * slots : (k + 1) * slots, :] = block[...]
    pre = jnp.dot(all_ref[:, :width], weight_ref[0], preferred_element_type=F32)
    cots = all_ref[:, width : width + inner].astype(F32)
    gate = all_ref[:, width + inner :][:, :1].astype(F32)
    sig = jax.nn.sigmoid(pre)
    gated = gate * sig
    dpre_ref[joined:, :] = (cots * gated * (1.0 + pre * (1.0 - sig))).astype(BF16)
    act_ref[...] = (gated * pre).astype(BF16)
    own_ref[...] = columns(all_ref.at[:, :width], lax.axis_index("dp"), share)


def share_kernel(sizes, *refs):
    experts, slots, groups, count = sizes
    pairs = experts // 2
    mine, theirs, acts = refs[:groups], refs[groups : 2 * groups], refs[2 * groups : 2 * groups + 2]
    outs = refs[2 * groups + 2 :]
    share = mine[0].shape[1]
    me = lax.axis_index("expert")
    for j, out in enumerate(outs):
        for r in range(2):
            here = slice(j * slots, (j + 1) * slots)
            out[r * slots : (r + 1) * slots, groups * share :] = acts[r][here]
    for g in range(groups):
        placed = []
        for block in (mine[g], theirs[g]):
            ids = block[count:, :count][:1].astype(F32).astype(jnp.int32)
            one_hot = placing_of(ids, me, 2, experts, slots).astype(BF16)
            placed.append(
                jnp.dot(one_hot, block[:count, :], preferred_element_type=F32).astype(BF16)
            )
        for j, out in enumerate(outs):
            here = slice(j * slots, (j + 1) * slots)
            out[:, g * share : (g + 1) * share] = jnp.concatenate([p[here] for p in placed], axis=0)


def split_kernel(slots, inner, *refs):
    *blocks, out_ref = refs
    for j, block in enumerate(blocks):
        out_ref[j * slots : (j + 1) * slots] = block[slots:, block.shape[1] - inner :]


def unplace_kernel(sizes, ids_ref, theirs_ref, *refs):
    experts, slots = sizes
    *blocks, out_ref = refs
    inner = out_ref.shape[1]
    me = lax.axis_index("expert")
    mine = [block[:slots, block.shape[1] - inner :] for block in blocks]
    total = jnp.zeros(out_ref.shape, F32)
    for r, value in enumerate((jnp.concatenate(mine, axis=0), theirs_ref[...])):
        one_hot = placing_of(ids_ref[...], me ^ r, 2, experts, slots).astype(BF16)
        total = total + lax.dot_general(
            one_hot, value, (((0,), (0,)), ((), ())), preferred_element_type=F32
        )
    out_ref[...] = total.astype(BF16)


def turn_kernel(groups, *refs):
    own, blocks, out_ref = refs[:2], refs[2:-1], refs[-1]
    share, rows = out_ref.shape[0], own[0].shape[0]
    slots = blocks[0].shape[0] // 2
    for r in range(2):
        out_ref[:, r * rows : (r + 1) * rows] = own[r][...].T
        for g in range(groups):
            value = [block[r * slots : (r + 1) * slots, g * share : (g + 1) * share] for block in blocks]
            at = (2 * g + 2 + r) * rows
            out_ref[:, at : at + rows] = jnp.concatenate(value, axis=0).T


def sum_kernel(groups, left_ref, *refs):
    pieces, (out_ref, right_ref) = refs[:-2], refs[-2:]
    rows = left_ref.shape[1] // 4
    at = 0
    for piece in pieces:
        right_ref[at : at + piece.shape[0], :] = piece[...]
        at += piece.shape[0]
    total = jnp.zeros(out_ref.shape, F32)
    for i, g in enumerate(groups):
        total = total + jnp.dot(
            left_ref[:, g * rows : (g + 1) * rows],
            right_ref[i * rows : (i + 1) * rows, :],
            preferred_element_type=F32,
        )
    out_ref[...] = total


def grad_kernel(group, left_ref, before_ref, *refs):
    pieces, (out_hbm, right_ref, total_ref, sems) = refs[:-4], refs[-4:]
    rows = left_ref.shape[1] // 4
    at = 0
    for piece in pieces:
        right_ref[at : at + piece.shape[0], :] = piece[...]
        at += piece.shape[0]
    steps, tall = total_ref.shape[:2]
    copies = []
    for i in range(steps):
        here = slice(i * tall, (i + 1) * tall)
        total_ref[i] = before_ref[here, :] + jnp.dot(
            left_ref[here, group * rows : (group + 1) * rows],
            right_ref[...],
            preferred_element_type=F32,
        )
        copies.append(pltpu.make_async_copy(total_ref.at[i], out_hbm.at[here, :], sems.at[i]))
        copies[-1].start()
    for copy in copies:
        copy.wait()


def on_device(tokens, expert_ids, gates, cotangent, weights):
    experts, members = lax.axis_size("expert"), lax.axis_size("dp")
    group = lax.axis_index("dp")
    pairs, groups = experts // 2, members - 1
    count, width = tokens.shape
    inner = cotangent.shape[1]
    share = width // members
    slots = max(2, 2 * count // experts)
    rows = experts * slots
    wide = width + inner + LANES
    chain = slots % 16 == 0 and share % LANES == 0 and members == 4
    ids, gates = expert_ids.reshape(1, count), gates.reshape(1, count)

    mine = (ids, gates, cotangent, tokens)
    placed = pl.pallas_call(
        functools.partial(place_kernel, (experts, slots)),
        out_shape=[struct(slots, wide)] * experts + [struct(count + TAIL, share)] * groups,
        in_specs=[HBM] * 4,
        out_specs=[VMEM] * (experts + groups),
        scratch_shapes=[pltpu.VMEM(value.shape, value.dtype) for value in mine]
        + [pltpu.SemaphoreType.DMA((4,))],
        compiler_params=limit(BIG),
        name="place",
    )(*mine)
    placed, cuts = placed[:experts], placed[experts:]
    touched = pl.pallas_call(
        touch_kernel,
        out_shape=struct(8, LANES),
        in_specs=[VMEM, ANY],
        out_specs=VMEM,
        compiler_params=limit(1),
        name="touch",
    )(weights, placed[0])
    got = list(placed)
    for k in range(2, experts, 2):
        got[k] = swap(placed[k], "expert", k)
    for k in range(3, experts, 2):
        got[k] = swap(after([placed[k]], got[{3: experts - 2, 5: 2, 7: 4}.get(k, 2)], *([touched] if k == 3 else []))[0], "expert", k)
    got[1] = swap(after([placed[1]], got[2])[0], "expert", 1)
    cuts = [swap(cut, "dp", k + 1) for k, cut in enumerate(cuts)]

    def forward(blocks, before, *ties):
        height = len(blocks) * slots
        joined = height + sum(value.shape[0] for value in before)
        return pl.pallas_call(
            functools.partial(forward_kernel, (len(blocks), width, inner, share)),
            out_shape=[struct(height, inner), struct(joined, inner), struct(height, share)],
            in_specs=[VMEM] * (1 + len(blocks) + len(before)) + [ANY] * len(ties),
            out_specs=[VMEM] * 3,
            scratch_shapes=[pltpu.VMEM((height, wide), BF16)],
            compiler_params=limit(SMALL),
            name="forward",
        )(weights, *blocks, *before, *ties)

    act, half, own = forward(got[::2], [], cuts[0])
    acts, owns = [act], [own]
    early = [swap(half, "dp", 3)] if chain else []
    crossed = [swap(cut, "expert", 1) for cut in cuts]
    act, dpre, own = forward(got[1::2], [half], *cuts, crossed[0])
    acts, owns, dpres = acts + [act], owns + [own], [dpre]
    gathered = [[] for _ in range(groups)]
    for k in reversed(range(1, members)):
        if chain and k == 3:
            gathered[2] = [*early, swap(dpre[rows // 2 :], "dp", 3)]
        elif not (chain and k == 2):
            gathered[k - 1].append(swap(dpre, "dp", k))
    if chain:
        ends = (group == 0) | (group == 3)
        value = jnp.where(ends, dpre, jnp.concatenate(gathered[2], axis=0))
        gathered[1].append(lax.ppermute(value, "dp", [(0, 2), (1, 0), (2, 3), (3, 1)]))

    sent = pl.pallas_call(
        functools.partial(share_kernel, (experts, slots, groups, count)),
        out_shape=[struct(2 * slots, groups * share + inner)] * pairs,
        in_specs=[VMEM] * (2 + 2 * groups),
        out_specs=[VMEM] * pairs,
        compiler_params=limit(SMALL),
        name="place_shares",
    )(*cuts, *crossed, *acts)
    lefts = [sent[0]] + [swap(sent[j], "expert", 2 * j) for j in range(1, pairs)]
    theirs = pl.pallas_call(
        functools.partial(split_kernel, slots, inner),
        out_shape=struct(pairs * slots, inner),
        in_specs=[VMEM] * pairs,
        out_specs=VMEM,
        compiler_params=limit(SMALL),
        name="split",
    )(*lefts)
    hidden = pl.pallas_call(
        functools.partial(unplace_kernel, (experts, slots)),
        out_shape=struct(count, inner),
        in_specs=[VMEM] * (2 + pairs),
        out_specs=VMEM,
        compiler_params=limit(SMALL),
        name="unplace",
    )(ids, swap(theirs, "expert", 1), *lefts)

    if chain:
        left = pl.pallas_call(
            functools.partial(turn_kernel, groups),
            out_shape=struct(share, members * rows),
            in_specs=[VMEM] * (2 + pairs),
            out_specs=VMEM,
            compiler_params=limit(SMALL),
            name="turn",
        )(*owns, *lefts)
        pieces = [*dpres] + gathered[0] + gathered[2]
        before = pl.pallas_call(
            functools.partial(sum_kernel, (0, 1, 3)),
            out_shape=jax.ShapeDtypeStruct((share, inner), F32),
            in_specs=[VMEM] * (1 + len(pieces)),
            out_specs=VMEM,
            scratch_shapes=[pltpu.VMEM((3 * rows, inner), BF16)],
            compiler_params=limit(SMALL),
            name="sum",
        )(left, *pieces)
        steps = 2
        grad = pl.pallas_call(
            functools.partial(grad_kernel, 2),
            out_shape=jax.ShapeDtypeStruct((share, inner), F32),
            in_specs=[VMEM] * (2 + len(dpres)),
            out_specs=HBM,
            scratch_shapes=[
                pltpu.VMEM((rows, inner), BF16),
                pltpu.VMEM((steps, share // steps, inner), F32),
                pltpu.SemaphoreType.DMA((steps,)),
            ],
            compiler_params=limit(SMALL),
            name="grad",
        )(left, before, *gathered[1])
        return (hidden, grad[None])
    left, right = list(owns), list(dpres)
    for g in range(groups):
        here = slice(g * share, (g + 1) * share)
        left += [b[r * slots : (r + 1) * slots, here] for r in range(2) for b in lefts]
        right += gathered[g]
    grad = lax.dot_general(
        jnp.concatenate(left, axis=0),
        jnp.concatenate(right, axis=0),
        (((0,), (0,)), ((), ())),
        preferred_element_type=F32,
    )
    return (hidden, grad[None])


BIG, SMALL, TOUCH, TIES = 40, 12, True, 1


def solution(mesh):
    return jax.shard_map(
        on_device,
        mesh=mesh,
        in_specs=(
            P(("dp", "expert"), None),
            P(("dp", "expert"), None),
            P(("dp", "expert")),
            P(("dp", "expert"), None),
            P("expert", None, None),
        ),
        out_specs=(P(("dp", "expert"), None), P("expert", "dp", None)),
        check_vma=False,
    )
```
